32 devices in a mesh: groups: 2 (over y), expert: 4 (over z), seq: 2 (over x), replica: 2 (over core).
Axes of the slice: x: 2, y: 2, z: 4, core: 2. Of those that a mesh axis runs over, the one named last changes fastest.
Arguments:
- tokens: bfloat16 [1024, 1024], P(('groups', 'expert', 'seq', 'replica')), parts along dimension 0, may hold values from -6 to 6
- cotangent: bfloat16 [1024, 1024], P(('groups', 'expert', 'seq', 'replica')), parts along dimension 0, may hold values from -6 to 6
- expert_ids: int32 [1024, 8], P(('groups', 'expert', 'seq', 'replica')), parts along dimension 0, may hold values from 0 to 7, as said below
- combine_int: int32 [1024, 8], P(('groups', 'expert', 'seq', 'replica')), parts along dimension 0, may hold values from 1 to 1023
- w_gate: bfloat16 [8, 1024, 384], P(('expert', 'seq')), may hold values from -0.1875 to 0.1875
- w_up: bfloat16 [8, 1024, 384], P(('expert', 'seq')), may hold values from -0.1875 to 0.1875
- w_down: bfloat16 [8, 384, 1024], P(('expert', 'seq')), may hold values from -0.3125 to 0.3125
Outputs:
- token_grad: bfloat16 [1024, 1024], P(('groups', 'expert', 'seq', 'replica')), parts along dimension 0
- combine_grad: float32 [1024, 8], P(('groups', 'expert', 'seq', 'replica')), parts along dimension 0
- grad_gate: float32 [16, 1024, 384], P(('groups', 'expert', 'seq'), 'replica'), parts along dimension 0
- grad_up: float32 [16, 1024, 384], P(('groups', 'expert', 'seq'), 'replica'), parts along dimension 0
The draws below stay inside these ranges and needn't reach their ends.
There are 2 independent parts, one for each index of `groups`. The reference program is written for one: setup_inputs(seed, part) draws one part's arguments, and reference() takes and returns one part's arrays. A program takes and returns all parts, laid end to end along the dimension named above; an argument that names none is the same for every part. Nothing has to cross between parts.
Inputs may be any that keep to these rules, and one draw needn't show every extreme that they name: `expert_ids`: each row names 8 different experts. The rows of one device name each expert at most 32 times, and some experts are named exactly 32 times by the rows of every device.
All inputs are finite; a program needn't handle non-finite values.
Results may differ from the reference program's by a relative error of at most 0.0065.
Values may be sent and summed in bfloat16 or wider, within the bound.
No kernel may reach another device: no remote copies, remote signals or barrier semaphores. Data moves between devices by JAX's collectives and lax.ppermute only.
A program may use at most 64 MiB of HBM per device.

```python
import jax
import jax.numpy as jnp
from jax import lax

D = 1024
H = 384
TOP = 8
TOK_DEV = 32
EXPERTS = 8
TOKENS = 512
CAP = 32


def draw_expert_ids(key, part):
    key = jax.random.fold_in(key, 11)
    stride = EXPERTS // TOP
    blocks = TOKENS // TOK_DEV
    leftover = TOK_DEV - CAP
    key_relabel, key_hot, key_rest, key_place, key_turn = jax.random.split(key, 5)
    relabel = jax.random.permutation(key_relabel, EXPERTS).astype(jnp.int32)
    hot_base = jax.random.randint(key_hot, (), 0, EXPERTS).astype(jnp.int32)
    values = jnp.arange(EXPERTS, dtype=jnp.int32)
    barred = values % stride == hot_base % stride
    scores = jax.random.randint(key_rest, (blocks, EXPERTS), 0, 2 ** 20).astype(jnp.int32) * EXPERTS + values[None, :]
    scores = jnp.where(barred[None, :], scores + 2 ** 28, scores)
    chosen = jnp.argsort(scores, axis=1)[:, :leftover].astype(jnp.int32)
    base_ids = jnp.concatenate([jnp.broadcast_to(hot_base, (blocks, CAP)).astype(jnp.int32), chosen], axis=1)
    place_keys = jax.random.split(key_place, blocks)
    places = jax.vmap(lambda single: jax.random.permutation(single, TOK_DEV))(place_keys).astype(jnp.int32)
    arranged = jnp.take_along_axis(base_ids, places, axis=1)
    rotation = jax.random.randint(key_turn, (blocks, TOK_DEV, 1), 0, TOP).astype(jnp.int32)
    offsets = (jnp.arange(TOP, dtype=jnp.int32)[None, None, :] + rotation) % TOP
    positions = (arranged[:, :, None] + offsets * stride) % EXPERTS
    return relabel[positions].reshape(TOKENS, TOP).astype(jnp.int32)


def touch_ends(values, key, smallest, top_value):
    extent = values.shape
    place = [jax.random.randint(jax.random.fold_in(key, axis), (), 0, extent[axis]) for axis in range(len(extent))]
    values = values.at[tuple(place)].set(smallest)
    longest = extent.index(max(extent))
    place[longest] = (place[longest] + 1) % extent[longest]
    return values.at[tuple(place)].set(top_value)


def levels(own_key, dims, pieces, least, high):
    def one(dim, parts):
        steps = jax.random.uniform(jax.random.fold_in(jax.random.fold_in(own_key, 6), dim), (parts,), jnp.float32, least / len(pieces), high / len(pieces))
        return jnp.repeat(jnp.exp(steps), dims[dim] // parts).reshape((-1,) + (1,) * (len(dims) - dim - 1))

    level = one(*pieces[0])
    for cut in pieces[1:]:
        level = level * one(*cut)
    return level


def noise(rng, extent, deviation, limit, shards=(), held_as=jnp.bfloat16):
    result = jax.random.normal(rng, extent, jnp.float32) * deviation
    if len(shards) > 0:
        result = levels(rng, extent, shards, -0.22, 0.18) * result
    return jnp.clip(result, min=-limit, max=limit).astype(held_as)


def setup_inputs(seed: int = 0, part: int = 0) -> dict:
    seeds = jax.random.split(jax.random.key(seed), 8)
    part_keys = jax.random.split(jax.random.fold_in(seeds[7], part), 8)
    tokens = noise(part_keys[0], (TOKENS, D), 1.0, 6.0, ((0, 16),))
    cotangent = noise(part_keys[1], (TOKENS, D), 0.5, 6.0, ((0, 16),))
    expert_ids = draw_expert_ids(jax.random.fold_in(jax.random.fold_in(seeds[7], part), 71), part)
    combine_int = touch_ends(jax.random.randint(part_keys[3], (TOKENS, TOP), 1, 1024), jax.random.fold_in(part_keys[3], 1), 1, 1023).astype(jnp.int32)
    w_gate = noise(seeds[4], (EXPERTS, D, H), D ** -0.5, 0.1875, ((0, 8),))
    w_up = noise(seeds[5], (EXPERTS, D, H), D ** -0.5, 0.1875, ((0, 8),))
    w_down = noise(seeds[6], (EXPERTS, H, D), H ** -0.5, 0.3125, ((0, 8),))
    return {"tokens": tokens, "cotangent": cotangent, "expert_ids": expert_ids, "combine_int": combine_int, "w_gate": w_gate, "w_up": w_up, "w_down": w_down}


def expert_pass(x_rows, y_rows, mix_rows, gate_w, up_w, down_w):
    pre_gate = jnp.dot(x_rows, gate_w, preferred_element_type=jnp.float32)
    pre_up = jnp.dot(x_rows, up_w, preferred_element_type=jnp.float32)
    back_hidden = lax.dot_general(y_rows, down_w, (((1,), (1,)), ((), ())), preferred_element_type=jnp.float32)
    sigmoid_gate = jax.nn.sigmoid(pre_gate)
    activated = pre_gate * sigmoid_gate
    hidden = activated * pre_up
    pair_comb = jnp.sum(back_hidden * hidden, axis=1).astype(jnp.bfloat16)
    scaled = mix_rows.astype(jnp.float32)[:, None] * back_hidden
    d_gate = (scaled * pre_up * sigmoid_gate * (1.0 + pre_gate * (1.0 - sigmoid_gate))).astype(jnp.bfloat16)
    d_up = (scaled * activated).astype(jnp.bfloat16)
    token_part = lax.dot_general(d_gate, gate_w, (((1,), (1,)), ((), ())), preferred_element_type=jnp.float32)
    token_part = token_part + lax.dot_general(d_up, up_w, (((1,), (1,)), ((), ())), preferred_element_type=jnp.float32)
    return d_gate, d_up, token_part.astype(jnp.bfloat16), pair_comb


def reference(tokens, cotangent, expert_ids, combine_int, w_gate, w_up, w_down):
    weights_f = combine_int.astype(jnp.float32)
    mix_weights = (weights_f / jnp.sum(weights_f, axis=1, keepdims=True)).astype(jnp.bfloat16)
    member = (expert_ids[:, :, None] == jnp.arange(EXPERTS, dtype=jnp.int32)[None, None, :]).astype(jnp.int32)
    per_token = jnp.sum(member, axis=1)
    earlier = jnp.cumsum(per_token, axis=0) - per_token
    rank_in = jnp.sum(earlier[:, None, :] * member, axis=2).astype(jnp.int32)
    capacity = TOKENS // TOK_DEV * CAP
    pair_index = jnp.arange(TOKENS * TOP, dtype=jnp.int32).reshape(TOKENS, TOP)
    slot_table = jnp.full((EXPERTS, capacity), TOKENS * TOP, jnp.int32).at[expert_ids, rank_in].set(pair_index)
    tokens_pad = jnp.concatenate([tokens, jnp.zeros((1, D), jnp.bfloat16)], axis=0)
    cotan_pad = jnp.concatenate([cotangent, jnp.zeros((1, D), jnp.bfloat16)], axis=0)
    mix_pad = jnp.concatenate([mix_weights.reshape(-1), jnp.zeros((1,), jnp.bfloat16)], axis=0)

    def one_expert(state_pair, inputs):
        token_acc, comb_acc = state_pair
        pair_ids, gate_w, up_w, down_w = inputs
        owners = (pair_ids // TOP).astype(jnp.int32)
        x_rows = tokens_pad[owners]
        y_rows = cotan_pad[owners]
        mix_rows = mix_pad[pair_ids]
        d_gate, d_up, token_part, pair_comb = expert_pass(x_rows, y_rows, mix_rows, gate_w, up_w, down_w)
        grad_g = lax.dot_general(x_rows, d_gate, (((0,), (0,)), ((), ())), preferred_element_type=jnp.float32)
        grad_u = lax.dot_general(x_rows, d_up, (((0,), (0,)), ((), ())), preferred_element_type=jnp.float32)
        token_acc = token_acc.at[owners].add(token_part.astype(jnp.float32))
        comb_acc = comb_acc.at[pair_ids].set(pair_comb.astype(jnp.float32))
        return (token_acc, comb_acc), (grad_g, grad_u)

    start_state = (jnp.zeros((TOKENS + 1, D), jnp.float32), jnp.zeros((TOKENS * TOP + 1,), jnp.float32))
    final_state, grad_pair = lax.scan(one_expert, start_state, (slot_table, w_gate, w_up, w_down))
    token_acc, comb_acc = final_state
    grad_gate, grad_up = grad_pair
    token_grad = token_acc[:TOKENS].astype(jnp.bfloat16)
    combine_grad = comb_acc[:TOKENS * TOP].reshape(TOKENS, TOP)
    return (token_grad, combine_grad, grad_gate, grad_up)
```

```python
import functools

import jax
import jax.numpy as jnp
from jax import lax
from jax.experimental import pallas as pl
from jax.experimental.pallas import tpu as pltpu
from jax.sharding import PartitionSpec as P

LANES = 128
VMEM_LIMIT = 32 * 1024 * 1024


def from_partner(block, axis, distance):
    count = lax.axis_size(axis)
    route = []
    for low in range(count):
        high = low | 1 << distance
        if high != low and high < count:
            route += [(low, high), (high, low)]
    return lax.ppermute(block, axis, route)


def expert_pass(x_rows, y_rows, mix_rows, gate_w, up_w, down_w):
    pre_gate = jnp.dot(x_rows, gate_w, preferred_element_type=jnp.float32)
    pre_up = jnp.dot(x_rows, up_w, preferred_element_type=jnp.float32)
    back_hidden = lax.dot_general(
        y_rows, down_w, (((1,), (1,)), ((), ())), preferred_element_type=jnp.float32
    )
    sigmoid_gate = jax.nn.sigmoid(pre_gate)
    activated = pre_gate * sigmoid_gate
    hidden = activated * pre_up
    pair_comb = jnp.sum(back_hidden * hidden, axis=1).astype(jnp.bfloat16)
    scaled = mix_rows.astype(jnp.float32)[:, None] * back_hidden
    d_gate = (scaled * pre_up * sigmoid_gate * (1.0 + pre_gate * (1.0 - sigmoid_gate))).astype(
        jnp.bfloat16
    )
    d_up = (scaled * activated).astype(jnp.bfloat16)
    token_part = lax.dot_general(
        d_gate, gate_w, (((1,), (1,)), ((), ())), preferred_element_type=jnp.float32
    )
    token_part = token_part + lax.dot_general(
        d_up, up_w, (((1,), (1,)), ((), ())), preferred_element_type=jnp.float32
    )
    return (d_gate, d_up, token_part.astype(jnp.bfloat16), pair_comb)


def routed_body(tokens, cotangent, expert_ids, combine_int, w_gate, w_up, w_down):
    peer_count = lax.axis_size(("expert", "seq"))
    count_tok, feature_dim = tokens.shape
    top_k = expert_ids.shape[1]
    hidden_w = w_gate.shape[2]
    capacity = min(count_tok, max(top_k, 4 * count_tok * top_k // peer_count))
    slots_all = peer_count * capacity
    weights_f = combine_int.astype(jnp.float32)
    mix_weights = (weights_f / jnp.sum(weights_f, axis=1, keepdims=True)).astype(jnp.bfloat16)
    member = (
        expert_ids[:, :, None] == jnp.arange(peer_count, dtype=jnp.int32)[None, None, :]
    ).astype(jnp.int32)
    per_token = jnp.sum(member, axis=1)
    earlier = jnp.cumsum(per_token, axis=0) - per_token
    rank_in = jnp.sum(earlier[:, None, :] * member, axis=2)
    slot_ids = expert_ids * capacity + rank_in
    routing = (
        slot_ids[:, :, None] == jnp.arange(slots_all, dtype=jnp.int32)[None, None, :]
    ).astype(jnp.float32)
    placing = jnp.sum(routing, axis=1).astype(jnp.bfloat16)
    sent_x = lax.dot_general(
        placing, tokens, (((0,), (0,)), ((), ())), preferred_element_type=jnp.float32
    )
    sent_x = sent_x.astype(jnp.bfloat16).reshape(peer_count, capacity, feature_dim)
    sent_y = lax.dot_general(
        placing, cotangent, (((0,), (0,)), ((), ())), preferred_element_type=jnp.float32
    )
    sent_y = sent_y.astype(jnp.bfloat16).reshape(peer_count, capacity, feature_dim)
    sent_g = jnp.einsum("tks,tk->s", routing, mix_weights.astype(jnp.float32))
    sent_g = sent_g.astype(jnp.bfloat16).reshape(peer_count, capacity)
    got_x, got_y, got_g = (
        lax.all_to_all(sent_x, ("expert", "seq"), split_axis=0, concat_axis=0, tiled=True),
        lax.all_to_all(sent_y, ("expert", "seq"), split_axis=0, concat_axis=0, tiled=True),
        lax.all_to_all(sent_g, ("expert", "seq"), split_axis=0, concat_axis=0, tiled=True),
    )
    x_rows = got_x.reshape(slots_all, feature_dim)
    y_rows = got_y.reshape(slots_all, feature_dim)
    mix_rows = got_g.reshape(slots_all)
    d_gate, d_up, token_part, pair_comb = expert_pass(
        x_rows, y_rows, mix_rows, w_gate[0], w_up[0], w_down[0]
    )
    ret_x, ret_c = (
        lax.all_to_all(
            token_part.reshape(peer_count, capacity, feature_dim),
            ("expert", "seq"),
            split_axis=0,
            concat_axis=0,
            tiled=True,
        ),
        lax.all_to_all(
            pair_comb.reshape(peer_count, capacity),
            ("expert", "seq"),
            split_axis=0,
            concat_axis=0,
            tiled=True,
        ),
    )
    d_both = jnp.concatenate([d_gate, d_up], axis=1)
    half_rows = feature_dim // lax.axis_size("replica")
    other_x, other_d = from_partner((x_rows, d_both), "replica", 0)
    first_row = lax.axis_index("replica") * half_rows
    own_cols = lax.dynamic_slice_in_dim(x_rows, first_row, half_rows, 1)
    other_cols = lax.dynamic_slice_in_dim(other_x, first_row, half_rows, 1)
    grad_rows = lax.dot_general(
        own_cols, d_both, (((0,), (0,)), ((), ())), preferred_element_type=jnp.float32
    )
    grad_rows = grad_rows + lax.dot_general(
        other_cols, other_d, (((0,), (0,)), ((), ())), preferred_element_type=jnp.float32
    )
    grad_gate = grad_rows[:, :hidden_w][None]
    grad_up = grad_rows[:, hidden_w:][None]
    token_grad = jnp.dot(
        placing, ret_x.reshape(slots_all, feature_dim), preferred_element_type=jnp.float32
    )
    combine_grad = jnp.einsum("tks,s->tk", routing, ret_c.reshape(slots_all).astype(jnp.float32))
    return (token_grad.astype(jnp.bfloat16), combine_grad, grad_gate, grad_up)


def call(kernel, out_shape, *operands, flops=0, moved=0, in_specs=None):
    return pl.pallas_call(
        kernel,
        out_shape=out_shape,
        in_specs=in_specs or [pl.BlockSpec(memory_space=pltpu.VMEM)] * len(operands),
        cost_estimate=pl.CostEstimate(flops=flops, bytes_accessed=moved, transcendentals=0),
        compiler_params=pltpu.CompilerParams(vmem_limit_bytes=VMEM_LIMIT),
    )(*operands)


def message_kernel(x_ref, y_ref, ids_ref, comb_ref, out_ref):
    feature_dim = x_ref.shape[1]
    out_ref[:, :feature_dim] = x_ref[...]
    out_ref[:, feature_dim : 2 * feature_dim] = y_ref[...]
    weights = comb_ref[...].astype(jnp.float32)
    mix = (weights / jnp.sum(weights, axis=1, keepdims=True)).astype(jnp.bfloat16)
    mix = mix.astype(jnp.float32)
    ids = ids_ref[...]
    lane = lax.broadcasted_iota(jnp.int32, (ids.shape[0], LANES), 1)
    by_expert = jnp.zeros(lane.shape, jnp.float32)
    for k in range(ids.shape[1]):
        by_expert += jnp.where(ids[:, k : k + 1] == lane, mix[:, k : k + 1], 0.0)
    out_ref[:, 2 * feature_dim :] = by_expert.astype(jnp.bfloat16)


def expert_kernel(place_ref, *refs):
    blocks = refs[:8]
    gate_ref, up_ref, down_ref = refs[8:11]
    part_refs = refs[11:19]
    swap_ref, keep_ref = refs[19:]
    rows, width = blocks[0].shape
    feature_dim = (width - LANES) // 2
    half = feature_dim // 2
    expert, replica = place_ref[0], place_ref[1]
    data = jnp.concatenate([block[...] for block in blocks], axis=0)
    x_rows = data[:, :feature_dim]
    y_rows = data[:, feature_dim : 2 * feature_dim]
    lane = lax.broadcasted_iota(jnp.int32, (8 * rows, LANES), 1)
    mix = jnp.sum(
        jnp.where(lane == expert, data[:, 2 * feature_dim :].astype(jnp.float32), 0.0),
        axis=1,
        keepdims=True,
    )
    gate_w, up_w = gate_ref[0], up_ref[0]
    nt = (((1,), (1,)), ((), ()))
    pre_gate = jnp.dot(x_rows, gate_w, preferred_element_type=jnp.float32)
    pre_up = jnp.dot(x_rows, up_w, preferred_element_type=jnp.float32)
    back = lax.dot_general(y_rows, down_ref[0], nt, preferred_element_type=jnp.float32)
    sig = jax.nn.sigmoid(pre_gate)
    activated = pre_gate * sig
    pair_comb = jnp.sum(back * (activated * pre_up), axis=1, keepdims=True)
    scaled = mix * back
    d_gate = (scaled * pre_up * sig * (1.0 + pre_gate * (1.0 - sig))).astype(jnp.bfloat16)
    d_up = (scaled * activated).astype(jnp.bfloat16)
    part = lax.dot_general(d_gate, gate_w, nt, preferred_element_type=jnp.float32)
    part += lax.dot_general(d_up, up_w, nt, preferred_element_type=jnp.float32)
    part = part.astype(jnp.bfloat16)
    comb = jnp.where(lane == expert, pair_comb, 0.0).astype(jnp.bfloat16)
    for index, out in enumerate(part_refs):
        out[:, :feature_dim] = part[index * rows : (index + 1) * rows]
        out[:, feature_dim:] = comb[index * rows : (index + 1) * rows]
    hidden_w = d_gate.shape[1]
    first, second = x_rows[:, :half], x_rows[:, half:]
    swap_ref[:, :half] = jnp.where(replica == 0, second, first)
    swap_ref[:, half : half + hidden_w] = d_gate
    swap_ref[:, half + hidden_w :] = d_up
    keep_ref[...] = jnp.where(replica == 0, first, second)


def weight_kernel(keep_ref, own_ref, other_ref, gate_ref, up_ref):
    half = keep_ref.shape[1]
    hidden_w = gate_ref.shape[2]
    cols = jnp.concatenate([keep_ref[...], other_ref[:, :half]], axis=0)
    grads = jnp.concatenate([own_ref[:, half:], other_ref[:, half:]], axis=0)
    total = lax.dot_general(
        cols, grads, (((0,), (0,)), ((), ())), preferred_element_type=jnp.float32
    )
    gate_ref[0] = total[:, :hidden_w]
    up_ref[0] = total[:, hidden_w:]


def finish_kernel(ids_ref, *refs):
    token_ref, comb_ref = refs[-2:]
    feature_dim = token_ref.shape[1]
    total = refs[0][...].astype(jnp.float32)
    for ref in refs[1:-2]:
        total += ref[...].astype(jnp.float32)
    token_ref[...] = total[:, :feature_dim].astype(jnp.bfloat16)
    comb = total[:, feature_dim:]
    ids = ids_ref[...]
    lane = lax.broadcasted_iota(jnp.int32, comb.shape, 1)
    slot = lax.broadcasted_iota(jnp.int32, comb_ref.shape, 1)
    out = jnp.zeros(comb_ref.shape, jnp.float32)
    for k in range(ids.shape[1]):
        value = jnp.sum(jnp.where(ids[:, k : k + 1] == lane, comb, 0.0), axis=1, keepdims=True)
        out += jnp.where(slot == k, value, 0.0)
    comb_ref[...] = out


def across(block, mask):
    peers = ("expert", "seq")
    return lax.ppermute(block, peers, [(i, i ^ mask) for i in range(lax.axis_size(peers))])


def dense_body(tokens, cotangent, expert_ids, combine_int, w_gate, w_up, w_down):
    along_x, near_z, far_z = 1, 2, 4
    rows, feature_dim = tokens.shape
    hidden_w = w_gate.shape[2]
    half = feature_dim // 2
    bf16, f32 = jnp.bfloat16, jnp.float32
    place = jnp.stack([lax.axis_index(("expert", "seq")), lax.axis_index("replica")])
    place = place.astype(jnp.int32)
    own = call(
        message_kernel,
        jax.ShapeDtypeStruct((rows, 2 * feature_dim + LANES), bf16),
        tokens,
        cotangent,
        expert_ids,
        combine_int,
        moved=8 * rows * feature_dim,
    )
    z2 = across(own, far_z)
    z1 = across(own, near_z)
    x0 = across(own, along_x)
    x1 = across(z1, along_x)
    z3 = across(z2, near_z)
    x2 = across(z2, along_x)
    x3 = across(x2, near_z)
    blocks = [own, z1, z2, z3, x0, x1, x2, x3]
    part = jax.ShapeDtypeStruct((rows, feature_dim + LANES), bf16)
    whole = pl.BlockSpec(memory_space=pltpu.VMEM)
    outs = call(
        expert_kernel,
        (part,) * 8
        + (
            jax.ShapeDtypeStruct((8 * rows, half + 2 * hidden_w), bf16),
            jax.ShapeDtypeStruct((8 * rows, half), bf16),
        ),
        place,
        *blocks,
        w_gate,
        w_up,
        w_down,
        flops=2 * 8 * rows * feature_dim * hidden_w * 5,
        moved=6 * feature_dim * hidden_w + 8 * rows * feature_dim * 8,
        in_specs=[pl.BlockSpec(memory_space=pltpu.SMEM)] + [whole] * 11,
    )
    parts, swap, keep = outs[:8], outs[8], outs[9]
    for_column, for_other = parts[:4], parts[4:]

    def add(a, b):
        return (a.astype(f32) + b.astype(f32)).astype(bf16)

    sum3 = add(for_column[3], across(for_other[3], along_x))
    r3 = across(sum3, near_z | far_z)
    sum2 = add(for_column[2], across(for_other[2], along_x))
    r2 = across(sum2, far_z)
    sum1 = add(for_column[1], across(for_other[1], along_x))
    r1 = across(sum1, near_z)
    r0 = across(for_other[0], along_x)
    other = lax.ppermute(swap, "replica", [(0, 1), (1, 0)])
    grad = jax.ShapeDtypeStruct((1, half, hidden_w), f32)
    grad_gate, grad_up = call(
        weight_kernel,
        (grad, grad),
        keep,
        swap,
        other,
        flops=2 * 16 * rows * half * 2 * hidden_w,
        moved=8 * half * hidden_w + 16 * rows * (half + 2 * hidden_w),
    )
    token_grad, combine_grad = call(
        finish_kernel,
        (
            jax.ShapeDtypeStruct((rows, feature_dim), bf16),
            jax.ShapeDtypeStruct(expert_ids.shape, f32),
        ),
        expert_ids,
        for_column[0],
        r0,
        r1,
        r2,
        r3,
        moved=12 * rows * feature_dim,
    )
    return (token_grad, combine_grad, grad_gate, grad_up)


def body(*operands):
    sizes = [lax.axis_size(name) for name in ("expert", "seq", "replica")]
    if sizes == [4, 2, 2] and operands[2].shape[1] == 8:
        return dense_body(*operands)
    return routed_body(*operands)


def solution(mesh):
    in_specs = (
        P(("groups", "expert", "seq", "replica"), None),
        P(("groups", "expert", "seq", "replica"), None),
        P(("groups", "expert", "seq", "replica"), None),
        P(("groups", "expert", "seq", "replica"), None),
        P(("expert", "seq"), None, None),
        P(("expert", "seq"), None, None),
        P(("expert", "seq"), None, None),
    )
    out_specs = (
        P(("groups", "expert", "seq", "replica"), None),
        P(("groups", "expert", "seq", "replica"), None),
        P(("groups", "expert", "seq"), "replica", None),
        P(("groups", "expert", "seq"), "replica", None),
    )
    return jax.shard_map(body, mesh=mesh, in_specs=in_specs, out_specs=out_specs, check_vma=False)
```

```python
import functools

import jax
import jax.numpy as jnp
from jax import lax
from jax.experimental import pallas as pl
from jax.experimental.pallas import tpu as pltpu
from jax.sharding import PartitionSpec as P

LANES = 128
VMEM_LIMIT = 32 * 1024 * 1024
VMEM_MOST = 56 * 1024 * 1024


def from_partner(block, axis, distance):
    count = lax.axis_size(axis)
    route = []
    for low in range(count):
        high = low | 1 << distance
        if high != low and high < count:
            route += [(low, high), (high, low)]
    return lax.ppermute(block, axis, route)


def expert_pass(x_rows, y_rows, mix_rows, gate_w, up_w, down_w):
    pre_gate = jnp.dot(x_rows, gate_w, preferred_element_type=jnp.float32)
    pre_up = jnp.dot(x_rows, up_w, preferred_element_type=jnp.float32)
    back_hidden = lax.dot_general(
        y_rows, down_w, (((1,), (1,)), ((), ())), preferred_element_type=jnp.float32
    )
    sigmoid_gate = jax.nn.sigmoid(pre_gate)
    activated = pre_gate * sigmoid_gate
    hidden = activated * pre_up
    pair_comb = jnp.sum(back_hidden * hidden, axis=1).astype(jnp.bfloat16)
    scaled = mix_rows.astype(jnp.float32)[:, None] * back_hidden
    d_gate = (scaled * pre_up * sigmoid_gate * (1.0 + pre_gate * (1.0 - sigmoid_gate))).astype(
        jnp.bfloat16
    )
    d_up = (scaled * activated).astype(jnp.bfloat16)
    token_part = lax.dot_general(
        d_gate, gate_w, (((1,), (1,)), ((), ())), preferred_element_type=jnp.float32
    )
    token_part = token_part + lax.dot_general(
        d_up, up_w, (((1,), (1,)), ((), ())), preferred_element_type=jnp.float32
    )
    return (d_gate, d_up, token_part.astype(jnp.bfloat16), pair_comb)


def routed_body(tokens, cotangent, expert_ids, combine_int, w_gate, w_up, w_down):
    peer_count = lax.axis_size(("expert", "seq"))
    count_tok, feature_dim = tokens.shape
    top_k = expert_ids.shape[1]
    hidden_w = w_gate.shape[2]
    capacity = min(count_tok, max(top_k, 4 * count_tok * top_k // peer_count))
    slots_all = peer_count * capacity
    weights_f = combine_int.astype(jnp.float32)
    mix_weights = (weights_f / jnp.sum(weights_f, axis=1, keepdims=True)).astype(jnp.bfloat16)
    member = (
        expert_ids[:, :, None] == jnp.arange(peer_count, dtype=jnp.int32)[None, None, :]
    ).astype(jnp.int32)
    per_token = jnp.sum(member, axis=1)
    earlier = jnp.cumsum(per_token, axis=0) - per_token
    rank_in = jnp.sum(earlier[:, None, :] * member, axis=2)
    slot_ids = expert_ids * capacity + rank_in
    routing = (
        slot_ids[:, :, None] == jnp.arange(slots_all, dtype=jnp.int32)[None, None, :]
    ).astype(jnp.float32)
    placing = jnp.sum(routing, axis=1).astype(jnp.bfloat16)
    sent_x = lax.dot_general(
        placing, tokens, (((0,), (0,)), ((), ())), preferred_element_type=jnp.float32
    )
    sent_x = sent_x.astype(jnp.bfloat16).reshape(peer_count, capacity, feature_dim)
    sent_y = lax.dot_general(
        placing, cotangent, (((0,), (0,)), ((), ())), preferred_element_type=jnp.float32
    )
    sent_y = sent_y.astype(jnp.bfloat16).reshape(peer_count, capacity, feature_dim)
    sent_g = jnp.einsum("tks,tk->s", routing, mix_weights.astype(jnp.float32))
    sent_g = sent_g.astype(jnp.bfloat16).reshape(peer_count, capacity)
    got_x, got_y, got_g = (
        lax.all_to_all(sent_x, ("expert", "seq"), split_axis=0, concat_axis=0, tiled=True),
        lax.all_to_all(sent_y, ("expert", "seq"), split_axis=0, concat_axis=0, tiled=True),
        lax.all_to_all(sent_g, ("expert", "seq"), split_axis=0, concat_axis=0, tiled=True),
    )
    x_rows = got_x.reshape(slots_all, feature_dim)
    y_rows = got_y.reshape(slots_all, feature_dim)
    mix_rows = got_g.reshape(slots_all)
    d_gate, d_up, token_part, pair_comb = expert_pass(
        x_rows, y_rows, mix_rows, w_gate[0], w_up[0], w_down[0]
    )
    ret_x, ret_c = (
        lax.all_to_all(
            token_part.reshape(peer_count, capacity, feature_dim),
            ("expert", "seq"),
            split_axis=0,
            concat_axis=0,
            tiled=True,
        ),
        lax.all_to_all(
            pair_comb.reshape(peer_count, capacity),
            ("expert", "seq"),
            split_axis=0,
            concat_axis=0,
            tiled=True,
        ),
    )
    d_both = jnp.concatenate([d_gate, d_up], axis=1)
    half_rows = feature_dim // lax.axis_size("replica")
    other_x, other_d = from_partner((x_rows, d_both), "replica", 0)
    first_row = lax.axis_index("replica") * half_rows
    own_cols = lax.dynamic_slice_in_dim(x_rows, first_row, half_rows, 1)
    other_cols = lax.dynamic_slice_in_dim(other_x, first_row, half_rows, 1)
    grad_rows = lax.dot_general(
        own_cols, d_both, (((0,), (0,)), ((), ())), preferred_element_type=jnp.float32
    )
    grad_rows = grad_rows + lax.dot_general(
        other_cols, other_d, (((0,), (0,)), ((), ())), preferred_element_type=jnp.float32
    )
    grad_gate = grad_rows[:, :hidden_w][None]
    grad_up = grad_rows[:, hidden_w:][None]
    token_grad = jnp.dot(
        placing, ret_x.reshape(slots_all, feature_dim), preferred_element_type=jnp.float32
    )
    combine_grad = jnp.einsum("tks,s->tk", routing, ret_c.reshape(slots_all).astype(jnp.float32))
    return (token_grad.astype(jnp.bfloat16), combine_grad, grad_gate, grad_up)


NT = (((1,), (1,)), ((), ()))
VMEM = pl.BlockSpec(memory_space=pltpu.VMEM)
SMEM = pl.BlockSpec(memory_space=pltpu.SMEM)
HBM = pl.BlockSpec(memory_space=pltpu.HBM)


def call(kernel, out_shape, *operands, in_specs, out_specs, scratch=(), flops=0, moved=0, limit=VMEM_LIMIT, aliases={}):
    return pl.pallas_call(
        kernel,
        out_shape=out_shape,
        in_specs=in_specs,
        out_specs=out_specs,
        scratch_shapes=scratch,
        input_output_aliases=aliases,
        cost_estimate=pl.CostEstimate(flops=flops, bytes_accessed=moved, transcendentals=0),
        compiler_params=pltpu.CompilerParams(vmem_limit_bytes=limit),
    )(*operands)


def one_hot_rows(rows):
    shape = (rows, rows)
    here = lax.broadcasted_iota(jnp.int32, shape, 0) == lax.broadcasted_iota(jnp.int32, shape, 1)
    return here.astype(jnp.bfloat16)


def message_kernel(x_ref, y_ref, ids_hbm, comb_hbm, out_ref, ids_ref, comb_ref, *sems):
    feature_dim = x_ref.shape[1]
    ids_sem, comb_sem, x_sem, y_sem = sems
    ids_copy = pltpu.make_async_copy(ids_hbm, ids_ref, ids_sem)
    comb_copy = pltpu.make_async_copy(comb_hbm, comb_ref, comb_sem)
    ids_copy.start()
    comb_copy.start()
    x_copy = pltpu.make_async_copy(x_ref, out_ref.at[:, :feature_dim], x_sem)
    y_copy = pltpu.make_async_copy(y_ref, out_ref.at[:, feature_dim : 2 * feature_dim], y_sem)
    x_copy.start()
    y_copy.start()
    ids_copy.wait()
    comb_copy.wait()
    weights = comb_ref[...].astype(jnp.float32)
    mix = (weights / jnp.sum(weights, axis=0, keepdims=True)).astype(jnp.bfloat16)
    mix = mix.astype(jnp.float32)
    ids = ids_ref[...]
    count = ids.shape[1]
    expert = lax.broadcasted_iota(jnp.int32, (LANES, count), 0)
    by_expert = jnp.zeros((LANES, count), jnp.float32)
    for k in range(ids.shape[0]):
        by_expert += jnp.where(ids[k : k + 1] == expert, mix[k : k + 1], 0.0)
    turned = lax.dot_general(
        one_hot_rows(count), by_expert.astype(jnp.bfloat16), NT, preferred_element_type=jnp.float32
    )
    out_ref[:, 2 * feature_dim :] = turned.astype(jnp.bfloat16)
    x_copy.wait()
    y_copy.wait()


def expert_kernel(place_ref, touched_ref, *refs):
    blocks, (gate_ref, up_ref, down_ref) = refs[:8], refs[8:11]
    part_refs, (swap_ref, keep_ref) = refs[11:18], refs[18:]
    rows, width = blocks[0].shape
    feature_dim = (width - LANES) // 2
    half = feature_dim // 2
    expert, replica = place_ref[0], place_ref[1]
    data = jnp.concatenate([block[...] for block in blocks], axis=0)
    x_rows = data[:, :feature_dim]
    y_rows = data[:, feature_dim : 2 * feature_dim]
    lane = lax.broadcasted_iota(jnp.int32, (data.shape[0], LANES), 1)
    mix = jnp.sum(
        jnp.where(lane == expert, data[:, 2 * feature_dim :].astype(jnp.float32), 0.0),
        axis=1,
        keepdims=True,
    )
    gate, up = gate_ref[0], up_ref[0]
    pre_gate = jnp.dot(x_rows, gate, preferred_element_type=jnp.float32)
    pre_up = jnp.dot(x_rows, up, preferred_element_type=jnp.float32)
    back = lax.dot_general(y_rows, down_ref[0], NT, preferred_element_type=jnp.float32)
    sig = jax.nn.sigmoid(pre_gate)
    activated = pre_gate * sig
    pair_comb = jnp.sum(back * (activated * pre_up), axis=1, keepdims=True)
    scaled = mix * back
    d_gate = (scaled * pre_up * sig * (1.0 + pre_gate * (1.0 - sig))).astype(jnp.bfloat16)
    d_up = (scaled * activated).astype(jnp.bfloat16)
    part = lax.dot_general(d_gate, gate, NT, preferred_element_type=jnp.float32)
    part += lax.dot_general(d_up, up, NT, preferred_element_type=jnp.float32)
    part = part.astype(jnp.bfloat16)
    comb = jnp.where(lane == expert, pair_comb, 0.0).astype(jnp.bfloat16)
    first = 0
    for out in part_refs:
        last = first + out.shape[0]
        out[:, :feature_dim] = part[first:last]
        out[:, feature_dim:] = comb[first:last]
        first = last
    hidden_w = d_gate.shape[1]
    low, high = x_rows[:, :half], x_rows[:, half:]
    swap_ref[:, :half] = jnp.where(replica == 0, high, low)
    swap_ref[:, half : half + hidden_w] = d_gate
    swap_ref[:, half + hidden_w :] = d_up
    keep_ref[...] = jnp.where(replica == 0, low, high)


def touch_kernel(after_ref, gate_ref, up_ref, down_ref, out_ref):
    out_ref[...] = jnp.zeros(out_ref.shape, out_ref.dtype)


def weight_kernel(keep_ref, own_ref, other_ref, gate_ref, up_ref, done_ref):
    done_ref[...] = jnp.zeros(done_ref.shape, done_ref.dtype)
    half = keep_ref.shape[1]
    hidden_w = gate_ref.shape[2]
    cols = jnp.concatenate([keep_ref[...], other_ref[:, :half]], axis=0)
    grads = jnp.concatenate([own_ref[:, half:], other_ref[:, half:]], axis=0)
    total = lax.dot_general(
        cols, grads, (((0,), (0,)), ((), ())), preferred_element_type=jnp.float32
    )
    gate_ref[0] = total[:, :hidden_w]
    up_ref[0] = total[:, hidden_w:]


def finish_kernel(ids_hbm, done_ref, *refs):
    *refs, ids_ref, ids_sem = refs
    ids_copy = pltpu.make_async_copy(ids_hbm, ids_ref, ids_sem)
    ids_copy.start()
    token_ref, comb_ref = refs[-2:]
    rows, feature_dim = token_ref.shape
    total = refs[0][...].astype(jnp.float32)
    for ref in refs[1:-2]:
        total += ref[...].astype(jnp.float32)
    token_ref[...] = total[:, :feature_dim].astype(jnp.bfloat16)
    comb = total[:, feature_dim:].astype(jnp.bfloat16)
    turned = lax.dot_general(
        one_hot_rows(LANES), comb, NT, preferred_element_type=jnp.float32
    )
    ids_copy.wait()
    ids = ids_ref[...]
    out = jnp.zeros(ids.shape, jnp.float32)
    for expert in range(ids.shape[0]):
        out += jnp.where(ids == expert, turned[expert : expert + 1], 0.0)
    comb_ref[...] = out


def across(block, mask):
    peers = ("expert", "seq")
    return lax.ppermute(block, peers, [(i, i ^ mask) for i in range(lax.axis_size(peers))])


def swapped(block):
    return lax.ppermute(block, "replica", [(0, 1), (1, 0)])


def add(*terms):
    total = terms[0].astype(jnp.float32)
    for term in terms[1:]:
        total = total + term.astype(jnp.float32)
    return total.astype(jnp.bfloat16)


def after(value, *others):
    return lax.optimization_barrier((value,) + others)[0]


def dense_body(tokens, cotangent, expert_ids, combine_int, w_gate, w_up, w_down):
    along_x, near_z, far_z = 1, 2, 4
    rows, feature_dim = tokens.shape
    hidden_w = w_gate.shape[2]
    half = feature_dim // 2
    bf16, f32 = jnp.bfloat16, jnp.float32
    place = jnp.stack([lax.axis_index(("expert", "seq")), lax.axis_index("replica")])
    place = place.astype(jnp.int32)
    ids_turned = expert_ids.T
    own = call(
        message_kernel,
        jax.ShapeDtypeStruct((rows, 2 * feature_dim + LANES), bf16),
        tokens,
        cotangent,
        ids_turned,
        combine_int.T,
        in_specs=[HBM] * 4,
        out_specs=VMEM,
        scratch=[pltpu.VMEM(ids_turned.shape, jnp.int32)] * 2 + [pltpu.SemaphoreType.DMA] * 4,
        moved=8 * rows * feature_dim,
        limit=VMEM_MOST,
    )
    z3 = across(own, near_z | far_z)
    x2 = across(own, along_x | far_z)
    z1 = across(own, near_z)
    x0 = across(own, along_x)
    x1 = across(z1, along_x)
    x3 = across(z3, along_x)
    z2 = across(z3, near_z)
    held = (w_gate, w_up, w_down)
    touched = call(
        touch_kernel,
        jax.ShapeDtypeStruct((8, LANES), f32),
        z3,
        w_gate,
        w_up,
        w_down,
        in_specs=[VMEM] * 4,
        out_specs=VMEM,
        moved=12 * feature_dim * hidden_w,
    )
    part = jax.ShapeDtypeStruct((rows, feature_dim + LANES), bf16)
    pair = jax.ShapeDtypeStruct((2 * rows, feature_dim + LANES), bf16)
    f0, f1, f2, f3, g01, g2, g3, swap, keep = call(
        expert_kernel,
        [part] * 4
        + [
            pair,
            part,
            part,
            jax.ShapeDtypeStruct((8 * rows, half + 2 * hidden_w), bf16),
            jax.ShapeDtypeStruct((8 * rows, half), bf16),
        ],
        place,
        touched,
        *(own, z1, z2, z3, x0, x1, x2, x3),
        *held,
        in_specs=[SMEM] + [VMEM] * 12,
        out_specs=[VMEM] * 9,
        flops=2 * 8 * rows * feature_dim * hidden_w * 5,
        moved=6 * feature_dim * hidden_w + 8 * rows * feature_dim * 8,
    )
    sum3 = add(f3, across(g3, along_x))
    r3 = across(sum3, near_z | far_z)
    sum2 = add(f2, across(g2, along_x))
    r2 = across(sum2, far_z)
    h01 = across(g01, along_x)
    r1 = across(add(f1, h01[rows:]), near_z)
    other = swapped(swap)
    grad = jax.ShapeDtypeStruct((1, half, hidden_w), f32)
    grad_gate, grad_up, weights_done = call(
        weight_kernel,
        (grad, grad, jax.ShapeDtypeStruct((8, LANES), f32)),
        keep,
        swap,
        other,
        in_specs=[VMEM] * 3,
        out_specs=[pl.BlockSpec((1, half, hidden_w))] * 2 + [VMEM],
        flops=2 * 16 * rows * half * 2 * hidden_w,
        moved=8 * half * hidden_w + 16 * rows * (half + 2 * hidden_w),
    )
    token_grad, comb_turned = call(
        finish_kernel,
        (jax.ShapeDtypeStruct((rows, feature_dim), bf16), jax.ShapeDtypeStruct(ids_turned.shape, f32)),
        ids_turned,
        weights_done,
        *(f0, h01[:rows], r1, r2, r3),
        in_specs=[HBM] + [VMEM] * 6,
        out_specs=[pl.BlockSpec(tokens.shape), pl.BlockSpec(ids_turned.shape)],
        scratch=[pltpu.VMEM(ids_turned.shape, jnp.int32), pltpu.SemaphoreType.DMA],
        moved=12 * rows * feature_dim,
    )
    return (token_grad, comb_turned.T, grad_gate, grad_up)


def body(*operands):
    sizes = [lax.axis_size(name) for name in ("expert", "seq", "replica")]
    if sizes == [4, 2, 2] and operands[2].shape[1] == 8:
        return dense_body(*operands)
    return routed_body(*operands)


def solution(mesh):
    in_specs = (
        P(("groups", "expert", "seq", "replica"), None),
        P(("groups", "expert", "seq", "replica"), None),
        P(("groups", "expert", "seq", "replica"), None),
        P(("groups", "expert", "seq", "replica"), None),
        P(("expert", "seq"), None, None),
        P(("expert", "seq"), None, None),
        P(("expert", "seq"), None, None),
    )
    out_specs = (
        P(("groups", "expert", "seq", "replica"), None),
        P(("groups", "expert", "seq", "replica"), None),
        P(("groups", "expert", "seq"), "replica", None),
        P(("groups", "expert", "seq"), "replica", None),
    )
    return jax.shard_map(body, mesh=mesh, in_specs=in_specs, out_specs=out_specs, check_vma=False)
```

```python
import functools

import jax
import jax.numpy as jnp
from jax import lax
from jax.experimental import pallas as pl
from jax.experimental.pallas import tpu as pltpu
from jax.sharding import PartitionSpec as P

LANES = 128
VMEM_LIMIT = 32 * 1024 * 1024
VMEM_MOST = 56 * 1024 * 1024


def from_partner(block, axis, distance):
    count = lax.axis_size(axis)
    route = []
    for low in range(count):
        high = low | 1 << distance
        if high != low and high < count:
            route += [(low, high), (high, low)]
    return lax.ppermute(block, axis, route)


def expert_pass(x_rows, y_rows, mix_rows, gate_w, up_w, down_w):
    pre_gate = jnp.dot(x_rows, gate_w, preferred_element_type=jnp.float32)
    pre_up = jnp.dot(x_rows, up_w, preferred_element_type=jnp.float32)
    back_hidden = lax.dot_general(
        y_rows, down_w, (((1,), (1,)), ((), ())), preferred_element_type=jnp.float32
    )
    sigmoid_gate = jax.nn.sigmoid(pre_gate)
    activated = pre_gate * sigmoid_gate
    hidden = activated * pre_up
    pair_comb = jnp.sum(back_hidden * hidden, axis=1).astype(jnp.bfloat16)
    scaled = mix_rows.astype(jnp.float32)[:, None] * back_hidden
    d_gate = (scaled * pre_up * sigmoid_gate * (1.0 + pre_gate * (1.0 - sigmoid_gate))).astype(
        jnp.bfloat16
    )
    d_up = (scaled * activated).astype(jnp.bfloat16)
    token_part = lax.dot_general(
        d_gate, gate_w, (((1,), (1,)), ((), ())), preferred_element_type=jnp.float32
    )
    token_part = token_part + lax.dot_general(
        d_up, up_w, (((1,), (1,)), ((), ())), preferred_element_type=jnp.float32
    )
    return (d_gate, d_up, token_part.astype(jnp.bfloat16), pair_comb)


def routed_body(tokens, cotangent, expert_ids, combine_int, w_gate, w_up, w_down):
    peer_count = lax.axis_size(("expert", "seq"))
    count_tok, feature_dim = tokens.shape
    top_k = expert_ids.shape[1]
    hidden_w = w_gate.shape[2]
    capacity = min(count_tok, max(top_k, 4 * count_tok * top_k // peer_count))
    slots_all = peer_count * capacity
    weights_f = combine_int.astype(jnp.float32)
    mix_weights = (weights_f / jnp.sum(weights_f, axis=1, keepdims=True)).astype(jnp.bfloat16)
    member = (
        expert_ids[:, :, None] == jnp.arange(peer_count, dtype=jnp.int32)[None, None, :]
    ).astype(jnp.int32)
    per_token = jnp.sum(member, axis=1)
    earlier = jnp.cumsum(per_token, axis=0) - per_token
    rank_in = jnp.sum(earlier[:, None, :] * member, axis=2)
    slot_ids = expert_ids * capacity + rank_in
    routing = (
        slot_ids[:, :, None] == jnp.arange(slots_all, dtype=jnp.int32)[None, None, :]
    ).astype(jnp.float32)
    placing = jnp.sum(routing, axis=1).astype(jnp.bfloat16)
    sent_x = lax.dot_general(
        placing, tokens, (((0,), (0,)), ((), ())), preferred_element_type=jnp.float32
    )
    sent_x = sent_x.astype(jnp.bfloat16).reshape(peer_count, capacity, feature_dim)
    sent_y = lax.dot_general(
        placing, cotangent, (((0,), (0,)), ((), ())), preferred_element_type=jnp.float32
    )
    sent_y = sent_y.astype(jnp.bfloat16).reshape(peer_count, capacity, feature_dim)
    sent_g = jnp.einsum("tks,tk->s", routing, mix_weights.astype(jnp.float32))
    sent_g = sent_g.astype(jnp.bfloat16).reshape(peer_count, capacity)
    got_x, got_y, got_g = (
        lax.all_to_all(sent_x, ("expert", "seq"), split_axis=0, concat_axis=0, tiled=True),
        lax.all_to_all(sent_y, ("expert", "seq"), split_axis=0, concat_axis=0, tiled=True),
        lax.all_to_all(sent_g, ("expert", "seq"), split_axis=0, concat_axis=0, tiled=True),
    )
    x_rows = got_x.reshape(slots_all, feature_dim)
    y_rows = got_y.reshape(slots_all, feature_dim)
    mix_rows = got_g.reshape(slots_all)
    d_gate, d_up, token_part, pair_comb = expert_pass(
        x_rows, y_rows, mix_rows, w_gate[0], w_up[0], w_down[0]
    )
    ret_x, ret_c = (
        lax.all_to_all(
            token_part.reshape(peer_count, capacity, feature_dim),
            ("expert", "seq"),
            split_axis=0,
            concat_axis=0,
            tiled=True,
        ),
        lax.all_to_all(
            pair_comb.reshape(peer_count, capacity),
            ("expert", "seq"),
            split_axis=0,
            concat_axis=0,
            tiled=True,
        ),
    )
    d_both = jnp.concatenate([d_gate, d_up], axis=1)
    half_rows = feature_dim // lax.axis_size("replica")
    other_x, other_d = from_partner((x_rows, d_both), "replica", 0)
    first_row = lax.axis_index("replica") * half_rows
    own_cols = lax.dynamic_slice_in_dim(x_rows, first_row, half_rows, 1)
    other_cols = lax.dynamic_slice_in_dim(other_x, first_row, half_rows, 1)
    grad_rows = lax.dot_general(
        own_cols, d_both, (((0,), (0,)), ((), ())), preferred_element_type=jnp.float32
    )
    grad_rows = grad_rows + lax.dot_general(
        other_cols, other_d, (((0,), (0,)), ((), ())), preferred_element_type=jnp.float32
    )
    grad_gate = grad_rows[:, :hidden_w][None]
    grad_up = grad_rows[:, hidden_w:][None]
    token_grad = jnp.dot(
        placing, ret_x.reshape(slots_all, feature_dim), preferred_element_type=jnp.float32
    )
    combine_grad = jnp.einsum("tks,s->tk", routing, ret_c.reshape(slots_all).astype(jnp.float32))
    return (token_grad.astype(jnp.bfloat16), combine_grad, grad_gate, grad_up)


NT = (((1,), (1,)), ((), ()))
VMEM = pl.BlockSpec(memory_space=pltpu.VMEM)
SMEM = pl.BlockSpec(memory_space=pltpu.SMEM)
HBM = pl.BlockSpec(memory_space=pltpu.HBM)


def call(kernel, out_shape, *operands, in_specs, out_specs, scratch=(), flops=0, moved=0, limit=VMEM_LIMIT, aliases={}):
    return pl.pallas_call(
        kernel,
        out_shape=out_shape,
        in_specs=in_specs,
        out_specs=out_specs,
        scratch_shapes=scratch,
        input_output_aliases=aliases,
        cost_estimate=pl.CostEstimate(flops=flops, bytes_accessed=moved, transcendentals=0),
        compiler_params=pltpu.CompilerParams(vmem_limit_bytes=limit),
    )(*operands)


def one_hot_rows(rows):
    shape = (rows, rows)
    here = lax.broadcasted_iota(jnp.int32, shape, 0) == lax.broadcasted_iota(jnp.int32, shape, 1)
    return here.astype(jnp.bfloat16)


def message_kernel(x_ref, y_ref, ids_hbm, comb_hbm, out_ref, ids_ref, comb_ref, *sems):
    feature_dim = x_ref.shape[1]
    ids_sem, comb_sem, x_sem, y_sem = sems
    ids_copy = pltpu.make_async_copy(ids_hbm, ids_ref, ids_sem)
    comb_copy = pltpu.make_async_copy(comb_hbm, comb_ref, comb_sem)
    ids_copy.start()
    comb_copy.start()
    x_copy = pltpu.make_async_copy(x_ref, out_ref.at[:, :feature_dim], x_sem)
    y_copy = pltpu.make_async_copy(y_ref, out_ref.at[:, feature_dim : 2 * feature_dim], y_sem)
    x_copy.start()
    y_copy.start()
    ids_copy.wait()
    comb_copy.wait()
    weights = comb_ref[...].astype(jnp.float32)
    mix = (weights / jnp.sum(weights, axis=0, keepdims=True)).astype(jnp.bfloat16)
    mix = mix.astype(jnp.float32)
    ids = ids_ref[...]
    count = ids.shape[1]
    expert = lax.broadcasted_iota(jnp.int32, (LANES, count), 0)
    by_expert = jnp.zeros((LANES, count), jnp.float32)
    for k in range(ids.shape[0]):
        by_expert += jnp.where(ids[k : k + 1] == expert, mix[k : k + 1], 0.0)
    turned = lax.dot_general(
        one_hot_rows(count), by_expert.astype(jnp.bfloat16), NT, preferred_element_type=jnp.float32
    )
    out_ref[:, 2 * feature_dim :] = turned.astype(jnp.bfloat16)
    x_copy.wait()
    y_copy.wait()


def expert_kernel(place_ref, touched_ref, *refs):
    blocks, (gate_ref, up_ref, down_ref) = refs[:8], refs[8:11]
    part_refs, (swap_ref, keep_ref) = refs[11:18], refs[18:]
    rows, width = blocks[0].shape
    feature_dim = (width - LANES) // 2
    half = feature_dim // 2
    expert, replica = place_ref[0], place_ref[1]
    data = jnp.concatenate([block[...] for block in blocks], axis=0)
    x_rows = data[:, :feature_dim]
    y_rows = data[:, feature_dim : 2 * feature_dim]
    lane = lax.broadcasted_iota(jnp.int32, (data.shape[0], LANES), 1)
    mix = jnp.sum(
        jnp.where(lane == expert, data[:, 2 * feature_dim :].astype(jnp.float32), 0.0),
        axis=1,
        keepdims=True,
    )
    gate, up = gate_ref[0], up_ref[0]
    pre_gate = jnp.dot(x_rows, gate, preferred_element_type=jnp.float32)
    pre_up = jnp.dot(x_rows, up, preferred_element_type=jnp.float32)
    back = lax.dot_general(y_rows, down_ref[0], NT, preferred_element_type=jnp.float32)
    sig = jax.nn.sigmoid(pre_gate)
    activated = pre_gate * sig
    pair_comb = jnp.sum(back * (activated * pre_up), axis=1, keepdims=True)
    scaled = mix * back
    d_gate = (scaled * pre_up * sig * (1.0 + pre_gate * (1.0 - sig))).astype(jnp.bfloat16)
    d_up = (scaled * activated).astype(jnp.bfloat16)
    part = lax.dot_general(d_gate, gate, NT, preferred_element_type=jnp.float32)
    part += lax.dot_general(d_up, up, NT, preferred_element_type=jnp.float32)
    part = part.astype(jnp.bfloat16)
    comb = jnp.where(lane == expert, pair_comb, 0.0).astype(jnp.bfloat16)
    first = 0
    for out in part_refs:
        last = first + out.shape[0]
        out[:, :feature_dim] = part[first:last]
        out[:, feature_dim:] = comb[first:last]
        first = last
    hidden_w = d_gate.shape[1]
    low, high = x_rows[:, :half], x_rows[:, half:]
    swap_ref[:, :half] = jnp.where(replica == 0, high, low)
    swap_ref[:, half : half + hidden_w] = d_gate
    swap_ref[:, half + hidden_w :] = d_up
    keep_ref[...] = jnp.where(replica == 0, low, high)


def touch_kernel(after_ref, gate_ref, up_ref, down_ref, out_ref):
    out_ref[...] = jnp.zeros(out_ref.shape, out_ref.dtype)


def weight_kernel(keep_ref, own_ref, other_ref, gate_ref, up_ref, done_ref):
    done_ref[...] = jnp.zeros(done_ref.shape, done_ref.dtype)
    half = keep_ref.shape[1]
    hidden_w = gate_ref.shape[2]
    cols = jnp.concatenate([keep_ref[...], other_ref[:, :half]], axis=0)
    grads = jnp.concatenate([own_ref[:, half:], other_ref[:, half:]], axis=0)
    total = lax.dot_general(
        cols, grads, (((0,), (0,)), ((), ())), preferred_element_type=jnp.float32
    )
    gate_ref[0] = total[:, :hidden_w]
    up_ref[0] = total[:, hidden_w:]


def finish_kernel(ids_hbm, done_ref, *refs):
    *refs, ids_ref, ids_sem = refs
    ids_copy = pltpu.make_async_copy(ids_hbm, ids_ref, ids_sem)
    ids_copy.start()
    token_ref, comb_ref = refs[-2:]
    rows, feature_dim = token_ref.shape
    total = refs[0][...].astype(jnp.float32)
    for ref in refs[1:-2]:
        total += ref[...].astype(jnp.float32)
    token_ref[...] = total[:, :feature_dim].astype(jnp.bfloat16)
    comb = total[:, feature_dim:].astype(jnp.bfloat16)
    turned = lax.dot_general(
        one_hot_rows(LANES), comb, NT, preferred_element_type=jnp.float32
    )
    ids_copy.wait()
    ids = ids_ref[...]
    out = jnp.zeros(ids.shape, jnp.float32)
    for expert in range(ids.shape[0]):
        out += jnp.where(ids == expert, turned[expert : expert + 1], 0.0)
    comb_ref[...] = out


def across(block, mask):
    peers = ("expert", "seq")
    return lax.ppermute(block, peers, [(i, i ^ mask) for i in range(lax.axis_size(peers))])


def swapped(block):
    return lax.ppermute(block, "replica", [(0, 1), (1, 0)])


def add(*terms):
    total = terms[0].astype(jnp.float32)
    for term in terms[1:]:
        total = total + term.astype(jnp.float32)
    return total.astype(jnp.bfloat16)


def after(value, *others):
    return lax.optimization_barrier((value,) + others)[0]


def dense_body(tokens, cotangent, expert_ids, combine_int, w_gate, w_up, w_down):
    along_x, near_z, far_z = 1, 2, 4
    rows, feature_dim = tokens.shape
    hidden_w = w_gate.shape[2]
    half = feature_dim // 2
    bf16, f32 = jnp.bfloat16, jnp.float32
    place = jnp.stack([lax.axis_index(("expert", "seq")), lax.axis_index("replica")])
    place = place.astype(jnp.int32)
    ids_turned = expert_ids.T
    own = call(
        message_kernel,
        jax.ShapeDtypeStruct((rows, 2 * feature_dim + LANES), bf16),
        tokens,
        cotangent,
        ids_turned,
        combine_int.T,
        in_specs=[HBM] * 4,
        out_specs=VMEM,
        scratch=[pltpu.VMEM(ids_turned.shape, jnp.int32)] * 2 + [pltpu.SemaphoreType.DMA] * 4,
        moved=8 * rows * feature_dim,
        limit=VMEM_MOST,
    )
    z3 = across(own, near_z | far_z)
    x2 = across(own, along_x | far_z)
    z1 = across(own, near_z)
    x0 = across(own, along_x)
    x1 = across(z1, along_x)
    x3 = across(z3, along_x)
    z2 = across(z3, near_z)
    held = (w_gate, w_up, w_down)
    touched = call(
        touch_kernel,
        jax.ShapeDtypeStruct((8, LANES), f32),
        x0,
        w_gate,
        w_up,
        w_down,
        in_specs=[VMEM] * 4,
        out_specs=VMEM,
        moved=12 * feature_dim * hidden_w,
    )
    part = jax.ShapeDtypeStruct((rows, feature_dim + LANES), bf16)
    pair = jax.ShapeDtypeStruct((2 * rows, feature_dim + LANES), bf16)
    f0, f1, f2, f3, g01, g2, g3, swap, keep = call(
        expert_kernel,
        [part] * 4
        + [
            pair,
            part,
            part,
            jax.ShapeDtypeStruct((8 * rows, half + 2 * hidden_w), bf16),
            jax.ShapeDtypeStruct((8 * rows, half), bf16),
        ],
        place,
        touched,
        *(own, z1, z2, z3, x0, x1, x2, x3),
        *held,
        in_specs=[SMEM] + [VMEM] * 12,
        out_specs=[VMEM] * 9,
        flops=2 * 8 * rows * feature_dim * hidden_w * 5,
        moved=6 * feature_dim * hidden_w + 8 * rows * feature_dim * 8,
    )
    sum3 = add(f3, across(g3, along_x))
    r3 = across(sum3, near_z | far_z)
    sum2 = add(f2, across(g2, along_x))
    r2 = across(sum2, far_z)
    h01 = across(g01, along_x)
    r1 = across(add(f1, h01[rows:]), near_z)
    other = swapped(swap)
    grad = jax.ShapeDtypeStruct((1, half, hidden_w), f32)
    grad_gate, grad_up, weights_done = call(
        weight_kernel,
        (grad, grad, jax.ShapeDtypeStruct((8, LANES), f32)),
        keep,
        swap,
        other,
        in_specs=[VMEM] * 3,
        out_specs=[pl.BlockSpec((1, half, hidden_w))] * 2 + [VMEM],
        flops=2 * 16 * rows * half * 2 * hidden_w,
        moved=8 * half * hidden_w + 16 * rows * (half + 2 * hidden_w),
    )
    token_grad, comb_turned = call(
        finish_kernel,
        (jax.ShapeDtypeStruct((rows, feature_dim), bf16), jax.ShapeDtypeStruct(ids_turned.shape, f32)),
        ids_turned,
        weights_done,
        *(f0, h01[:rows], r1, r2, r3),
        in_specs=[HBM] + [VMEM] * 6,
        out_specs=[pl.BlockSpec(tokens.shape), pl.BlockSpec(ids_turned.shape)],
        scratch=[pltpu.VMEM(ids_turned.shape, jnp.int32), pltpu.SemaphoreType.DMA],
        moved=12 * rows * feature_dim,
    )
    return (token_grad, comb_turned.T, grad_gate, grad_up)


def body(*operands):
    sizes = [lax.axis_size(name) for name in ("expert", "seq", "replica")]
    if sizes == [4, 2, 2] and operands[2].shape[1] == 8:
        return dense_body(*operands)
    return routed_body(*operands)


def solution(mesh):
    in_specs = (
        P(("groups", "expert", "seq", "replica"), None),
        P(("groups", "expert", "seq", "replica"), None),
        P(("groups", "expert", "seq", "replica"), None),
        P(("groups", "expert", "seq", "replica"), None),
        P(("expert", "seq"), None, None),
        P(("expert", "seq"), None, None),
        P(("expert", "seq"), None, None),
    )
    out_specs = (
        P(("groups", "expert", "seq", "replica"), None),
        P(("groups", "expert", "seq", "replica"), None),
        P(("groups", "expert", "seq"), "replica", None),
        P(("groups", "expert", "seq"), "replica", None),
    )
    return jax.shard_map(body, mesh=mesh, in_specs=in_specs, out_specs=out_specs, check_vma=False)
```

```python
import functools

import jax
import jax.numpy as jnp
from jax import lax
from jax.experimental import pallas as pl
from jax.experimental.pallas import tpu as pltpu
from jax.sharding import PartitionSpec as P

LANES = 128
VMEM_LIMIT = 32 * 1024 * 1024
VMEM_MOST = 56 * 1024 * 1024


def from_partner(block, axis, distance):
    count = lax.axis_size(axis)
    route = []
    for low in range(count):
        high = low | 1 << distance
        if high != low and high < count:
            route += [(low, high), (high, low)]
    return lax.ppermute(block, axis, route)


def expert_pass(x_rows, y_rows, mix_rows, gate_w, up_w, down_w):
    pre_gate = jnp.dot(x_rows, gate_w, preferred_element_type=jnp.float32)
    pre_up = jnp.dot(x_rows, up_w, preferred_element_type=jnp.float32)
    back_hidden = lax.dot_general(
        y_rows, down_w, (((1,), (1,)), ((), ())), preferred_element_type=jnp.float32
    )
    sigmoid_gate = jax.nn.sigmoid(pre_gate)
    activated = pre_gate * sigmoid_gate
    hidden = activated * pre_up
    pair_comb = jnp.sum(back_hidden * hidden, axis=1).astype(jnp.bfloat16)
    scaled = mix_rows.astype(jnp.float32)[:, None] * back_hidden
    d_gate = (scaled * pre_up * sigmoid_gate * (1.0 + pre_gate * (1.0 - sigmoid_gate))).astype(
        jnp.bfloat16
    )
    d_up = (scaled * activated).astype(jnp.bfloat16)
    token_part = lax.dot_general(
        d_gate, gate_w, (((1,), (1,)), ((), ())), preferred_element_type=jnp.float32
    )
    token_part = token_part + lax.dot_general(
        d_up, up_w, (((1,), (1,)), ((), ())), preferred_element_type=jnp.float32
    )
    return (d_gate, d_up, token_part.astype(jnp.bfloat16), pair_comb)


def routed_body(tokens, cotangent, expert_ids, combine_int, w_gate, w_up, w_down):
    peer_count = lax.axis_size(("expert", "seq"))
    count_tok, feature_dim = tokens.shape
    top_k = expert_ids.shape[1]
    hidden_w = w_gate.shape[2]
    capacity = min(count_tok, max(top_k, 4 * count_tok * top_k // peer_count))
    slots_all = peer_count * capacity
    weights_f = combine_int.astype(jnp.float32)
    mix_weights = (weights_f / jnp.sum(weights_f, axis=1, keepdims=True)).astype(jnp.bfloat16)
    member = (
        expert_ids[:, :, None] == jnp.arange(peer_count, dtype=jnp.int32)[None, None, :]
    ).astype(jnp.int32)
    per_token = jnp.sum(member, axis=1)
    earlier = jnp.cumsum(per_token, axis=0) - per_token
    rank_in = jnp.sum(earlier[:, None, :] * member, axis=2)
    slot_ids = expert_ids * capacity + rank_in
    routing = (
        slot_ids[:, :, None] == jnp.arange(slots_all, dtype=jnp.int32)[None, None, :]
    ).astype(jnp.float32)
    placing = jnp.sum(routing, axis=1).astype(jnp.bfloat16)
    sent_x = lax.dot_general(
        placing, tokens, (((0,), (0,)), ((), ())), preferred_element_type=jnp.float32
    )
    sent_x = sent_x.astype(jnp.bfloat16).reshape(peer_count, capacity, feature_dim)
    sent_y = lax.dot_general(
        placing, cotangent, (((0,), (0,)), ((), ())), preferred_element_type=jnp.float32
    )
    sent_y = sent_y.astype(jnp.bfloat16).reshape(peer_count, capacity, feature_dim)
    sent_g = jnp.einsum("tks,tk->s", routing, mix_weights.astype(jnp.float32))
    sent_g = sent_g.astype(jnp.bfloat16).reshape(peer_count, capacity)
    got_x, got_y, got_g = (
        lax.all_to_all(sent_x, ("expert", "seq"), split_axis=0, concat_axis=0, tiled=True),
        lax.all_to_all(sent_y, ("expert", "seq"), split_axis=0, concat_axis=0, tiled=True),
        lax.all_to_all(sent_g, ("expert", "seq"), split_axis=0, concat_axis=0, tiled=True),
    )
    x_rows = got_x.reshape(slots_all, feature_dim)
    y_rows = got_y.reshape(slots_all, feature_dim)
    mix_rows = got_g.reshape(slots_all)
    d_gate, d_up, token_part, pair_comb = expert_pass(
        x_rows, y_rows, mix_rows, w_gate[0], w_up[0], w_down[0]
    )
    ret_x, ret_c = (
        lax.all_to_all(
            token_part.reshape(peer_count, capacity, feature_dim),
            ("expert", "seq"),
            split_axis=0,
            concat_axis=0,
            tiled=True,
        ),
        lax.all_to_all(
            pair_comb.reshape(peer_count, capacity),
            ("expert", "seq"),
            split_axis=0,
            concat_axis=0,
            tiled=True,
        ),
    )
    d_both = jnp.concatenate([d_gate, d_up], axis=1)
    half_rows = feature_dim // lax.axis_size("replica")
    other_x, other_d = from_partner((x_rows, d_both), "replica", 0)
    first_row = lax.axis_index("replica") * half_rows
    own_cols = lax.dynamic_slice_in_dim(x_rows, first_row, half_rows, 1)
    other_cols = lax.dynamic_slice_in_dim(other_x, first_row, half_rows, 1)
    grad_rows = lax.dot_general(
        own_cols, d_both, (((0,), (0,)), ((), ())), preferred_element_type=jnp.float32
    )
    grad_rows = grad_rows + lax.dot_general(
        other_cols, other_d, (((0,), (0,)), ((), ())), preferred_element_type=jnp.float32
    )
    grad_gate = grad_rows[:, :hidden_w][None]
    grad_up = grad_rows[:, hidden_w:][None]
    token_grad = jnp.dot(
        placing, ret_x.reshape(slots_all, feature_dim), preferred_element_type=jnp.float32
    )
    combine_grad = jnp.einsum("tks,s->tk", routing, ret_c.reshape(slots_all).astype(jnp.float32))
    return (token_grad.astype(jnp.bfloat16), combine_grad, grad_gate, grad_up)


NT = (((1,), (1,)), ((), ()))
VMEM = pl.BlockSpec(memory_space=pltpu.VMEM)
SMEM = pl.BlockSpec(memory_space=pltpu.SMEM)
HBM = pl.BlockSpec(memory_space=pltpu.HBM)


def call(kernel, out_shape, *operands, in_specs, out_specs, scratch=(), flops=0, moved=0, limit=VMEM_LIMIT, aliases={}):
    return pl.pallas_call(
        kernel,
        out_shape=out_shape,
        in_specs=in_specs,
        out_specs=out_specs,
        scratch_shapes=scratch,
        input_output_aliases=aliases,
        cost_estimate=pl.CostEstimate(flops=flops, bytes_accessed=moved, transcendentals=0),
        compiler_params=pltpu.CompilerParams(vmem_limit_bytes=limit),
    )(*operands)


def one_hot_rows(rows):
    shape = (rows, rows)
    here = lax.broadcasted_iota(jnp.int32, shape, 0) == lax.broadcasted_iota(jnp.int32, shape, 1)
    return here.astype(jnp.bfloat16)


def message_kernel(x_ref, y_ref, ids_hbm, comb_hbm, out_ref, ids_ref, comb_ref, *sems):
    feature_dim = x_ref.shape[1]
    ids_sem, comb_sem, x_sem, y_sem = sems
    ids_copy = pltpu.make_async_copy(ids_hbm, ids_ref, ids_sem)
    comb_copy = pltpu.make_async_copy(comb_hbm, comb_ref, comb_sem)
    ids_copy.start()
    comb_copy.start()
    x_copy = pltpu.make_async_copy(x_ref, out_ref.at[:, :feature_dim], x_sem)
    y_copy = pltpu.make_async_copy(y_ref, out_ref.at[:, feature_dim : 2 * feature_dim], y_sem)
    x_copy.start()
    y_copy.start()
    ids_copy.wait()
    comb_copy.wait()
    weights = comb_ref[...].astype(jnp.float32)
    mix = (weights / jnp.sum(weights, axis=0, keepdims=True)).astype(jnp.bfloat16)
    mix = mix.astype(jnp.float32)
    ids = ids_ref[...]
    count = ids.shape[1]
    expert = lax.broadcasted_iota(jnp.int32, (LANES, count), 0)
    by_expert = jnp.zeros((LANES, count), jnp.float32)
    for k in range(ids.shape[0]):
        by_expert += jnp.where(ids[k : k + 1] == expert, mix[k : k + 1], 0.0)
    turned = lax.dot_general(
        one_hot_rows(count), by_expert.astype(jnp.bfloat16), NT, preferred_element_type=jnp.float32
    )
    out_ref[:, 2 * feature_dim :] = turned.astype(jnp.bfloat16)
    x_copy.wait()
    y_copy.wait()


def expert_kernel(place_ref, touched_ref, *refs):
    blocks, (gate_ref, up_ref, down_ref) = refs[:8], refs[8:11]
    part_refs, (swap_ref, keep_ref) = refs[11:18], refs[18:]
    rows, width = blocks[0].shape
    feature_dim = (width - LANES) // 2
    half = feature_dim // 2
    expert, replica = place_ref[0], place_ref[1]
    data = jnp.concatenate([block[...] for block in blocks], axis=0)
    x_rows = data[:, :feature_dim]
    y_rows = data[:, feature_dim : 2 * feature_dim]
    lane = lax.broadcasted_iota(jnp.int32, (data.shape[0], LANES), 1)
    mix = jnp.sum(
        jnp.where(lane == expert, data[:, 2 * feature_dim :].astype(jnp.float32), 0.0),
        axis=1,
        keepdims=True,
    )
    gate, up = gate_ref[0], up_ref[0]
    pre_gate = jnp.dot(x_rows, gate, preferred_element_type=jnp.float32)
    pre_up = jnp.dot(x_rows, up, preferred_element_type=jnp.float32)
    back = lax.dot_general(y_rows, down_ref[0], NT, preferred_element_type=jnp.float32)
    sig = jax.nn.sigmoid(pre_gate)
    activated = pre_gate * sig
    pair_comb = jnp.sum(back * (activated * pre_up), axis=1, keepdims=True)
    scaled = mix * back
    d_gate = (scaled * pre_up * sig * (1.0 + pre_gate * (1.0 - sig))).astype(jnp.bfloat16)
    d_up = (scaled * activated).astype(jnp.bfloat16)
    part = lax.dot_general(d_gate, gate, NT, preferred_element_type=jnp.float32)
    part += lax.dot_general(d_up, up, NT, preferred_element_type=jnp.float32)
    part = part.astype(jnp.bfloat16)
    comb = jnp.where(lane == expert, pair_comb, 0.0).astype(jnp.bfloat16)
    first = 0
    for out in part_refs:
        last = first + out.shape[0]
        out[:, :feature_dim] = part[first:last]
        out[:, feature_dim:] = comb[first:last]
        first = last
    hidden_w = d_gate.shape[1]
    low, high = x_rows[:, :half], x_rows[:, half:]
    swap_ref[:, :half] = jnp.where(replica == 0, high, low)
    swap_ref[:, half : half + hidden_w] = d_gate
    swap_ref[:, half + hidden_w :] = d_up
    keep_ref[...] = jnp.where(replica == 0, low, high)


def touch_kernel(after_ref, gate_ref, up_ref, down_ref, out_ref):
    out_ref[...] = jnp.zeros(out_ref.shape, out_ref.dtype)


def weight_kernel(keep_ref, own_ref, other_ref, gate_ref, up_ref, done_ref):
    done_ref[...] = jnp.zeros(done_ref.shape, done_ref.dtype)
    half = keep_ref.shape[1]
    hidden_w = gate_ref.shape[2]
    cols = jnp.concatenate([keep_ref[...], other_ref[:, :half]], axis=0)
    grads = jnp.concatenate([own_ref[:, half:], other_ref[:, half:]], axis=0)
    total = lax.dot_general(
        cols, grads, (((0,), (0,)), ((), ())), preferred_element_type=jnp.float32
    )
    gate_ref[0] = total[:, :hidden_w]
    up_ref[0] = total[:, hidden_w:]


def finish_kernel(ids_hbm, done_ref, *refs):
    *refs, ids_ref, ids_sem = refs
    ids_copy = pltpu.make_async_copy(ids_hbm, ids_ref, ids_sem)
    ids_copy.start()
    token_ref, comb_ref = refs[-2:]
    rows, feature_dim = token_ref.shape
    total = refs[0][...].astype(jnp.float32)
    for ref in refs[1:-2]:
        total += ref[...].astype(jnp.float32)
    token_ref[...] = total[:, :feature_dim].astype(jnp.bfloat16)
    comb = total[:, feature_dim:].astype(jnp.bfloat16)
    turned = lax.dot_general(
        one_hot_rows(LANES), comb, NT, preferred_element_type=jnp.float32
    )
    ids_copy.wait()
    ids = ids_ref[...]
    out = jnp.zeros(ids.shape, jnp.float32)
    for expert in range(ids.shape[0]):
        out += jnp.where(ids == expert, turned[expert : expert + 1], 0.0)
    comb_ref[...] = out


def across(block, mask):
    peers = ("expert", "seq")
    return lax.ppermute(block, peers, [(i, i ^ mask) for i in range(lax.axis_size(peers))])


def swapped(block):
    return lax.ppermute(block, "replica", [(0, 1), (1, 0)])


def add(*terms):
    total = terms[0].astype(jnp.float32)
    for term in terms[1:]:
        total = total + term.astype(jnp.float32)
    return total.astype(jnp.bfloat16)


def after(value, *others):
    return lax.optimization_barrier((value,) + others)[0]


def dense_body(tokens, cotangent, expert_ids, combine_int, w_gate, w_up, w_down):
    along_x, near_z, far_z = 1, 2, 4
    rows, feature_dim = tokens.shape
    hidden_w = w_gate.shape[2]
    half = feature_dim // 2
    bf16, f32 = jnp.bfloat16, jnp.float32
    place = jnp.stack([lax.axis_index(("expert", "seq")), lax.axis_index("replica")])
    place = place.astype(jnp.int32)
    ids_turned = expert_ids.T
    own = call(
        message_kernel,
        jax.ShapeDtypeStruct((rows, 2 * feature_dim + LANES), bf16),
        tokens,
        cotangent,
        ids_turned,
        combine_int.T,
        in_specs=[HBM] * 4,
        out_specs=VMEM,
        scratch=[pltpu.VMEM(ids_turned.shape, jnp.int32)] * 2 + [pltpu.SemaphoreType.DMA] * 4,
        moved=8 * rows * feature_dim,
        limit=VMEM_MOST,
    )
    z3 = across(own, near_z | far_z)
    x2 = across(own, along_x | far_z)
    z1 = across(own, near_z)
    x0 = across(own, along_x)
    x1 = across(z1, along_x)
    x3 = across(z3, along_x)
    z2 = across(z3, near_z)
    held = (w_gate, w_up, w_down)
    touched = call(
        touch_kernel,
        jax.ShapeDtypeStruct((8, LANES), f32),
        x0,
        w_gate,
        w_up,
        w_down,
        in_specs=[VMEM] * 4,
        out_specs=VMEM,
        moved=12 * feature_dim * hidden_w,
    )
    part = jax.ShapeDtypeStruct((rows, feature_dim + LANES), bf16)
    pair = jax.ShapeDtypeStruct((2 * rows, feature_dim + LANES), bf16)
    f0, fg1, f2, f3, g0, g2, g3, swap, keep = call(
        expert_kernel,
        [part, pair]
        + [part] * 5
        + [
            jax.ShapeDtypeStruct((8 * rows, half + 2 * hidden_w), bf16),
            jax.ShapeDtypeStruct((8 * rows, half), bf16),
        ],
        place,
        touched,
        *(own, z1, x1, z2, z3, x0, x2, x3),
        *held,
        in_specs=[SMEM] + [VMEM] * 12,
        out_specs=[VMEM] * 9,
        flops=2 * 8 * rows * feature_dim * hidden_w * 5,
        moved=6 * feature_dim * hidden_w + 8 * rows * feature_dim * 8,
    )
    sum3 = add(f3, across(g3, along_x))
    r3 = across(sum3, near_z | far_z)
    sum2 = add(f2, across(g2, along_x))
    r2 = across(sum2, far_z)
    r1 = across(fg1, near_z)
    r0 = across(add(g0, r1[rows:]), along_x)
    other = swapped(swap)
    grad = jax.ShapeDtypeStruct((1, half, hidden_w), f32)
    grad_gate, grad_up, weights_done = call(
        weight_kernel,
        (grad, grad, jax.ShapeDtypeStruct((8, LANES), f32)),
        keep,
        swap,
        other,
        in_specs=[VMEM] * 3,
        out_specs=[pl.BlockSpec((1, half, hidden_w))] * 2 + [VMEM],
        flops=2 * 16 * rows * half * 2 * hidden_w,
        moved=8 * half * hidden_w + 16 * rows * (half + 2 * hidden_w),
    )
    token_grad, comb_turned = call(
        finish_kernel,
        (jax.ShapeDtypeStruct((rows, feature_dim), bf16), jax.ShapeDtypeStruct(ids_turned.shape, f32)),
        ids_turned,
        weights_done,
        *(f0, r1[:rows], r0, r2, r3),
        in_specs=[HBM] + [VMEM] * 6,
        out_specs=[pl.BlockSpec(tokens.shape), pl.BlockSpec(ids_turned.shape)],
        scratch=[pltpu.VMEM(ids_turned.shape, jnp.int32), pltpu.SemaphoreType.DMA],
        moved=12 * rows * feature_dim,
    )
    return (token_grad, comb_turned.T, grad_gate, grad_up)


def body(*operands):
    sizes = [lax.axis_size(name) for name in ("expert", "seq", "replica")]
    if sizes == [4, 2, 2] and operands[2].shape[1] == 8:
        return dense_body(*operands)
    return routed_body(*operands)


def solution(mesh):
    in_specs = (
        P(("groups", "expert", "seq", "replica"), None),
        P(("groups", "expert", "seq", "replica"), None),
        P(("groups", "expert", "seq", "replica"), None),
        P(("groups", "expert", "seq", "replica"), None),
        P(("expert", "seq"), None, None),
        P(("expert", "seq"), None, None),
        P(("expert", "seq"), None, None),
    )
    out_specs = (
        P(("groups", "expert", "seq", "replica"), None),
        P(("groups", "expert", "seq", "replica"), None),
        P(("groups", "expert", "seq"), "replica", None),
        P(("groups", "expert", "seq"), "replica", None),
    )
    return jax.shard_map(body, mesh=mesh, in_specs=in_specs, out_specs=out_specs, check_vma=False)
```

```python
import functools

import jax
import jax.numpy as jnp
from jax import lax
from jax.experimental import pallas as pl
from jax.experimental.pallas import tpu as pltpu
from jax.sharding import PartitionSpec as P

LANES = 128
VMEM_LIMIT = 32 * 1024 * 1024
VMEM_MOST = 56 * 1024 * 1024


def from_partner(block, axis, distance):
    count = lax.axis_size(axis)
    route = []
    for low in range(count):
        high = low | 1 << distance
        if high != low and high < count:
            route += [(low, high), (high, low)]
    return lax.ppermute(block, axis, route)


def expert_pass(x_rows, y_rows, mix_rows, gate_w, up_w, down_w):
    pre_gate = jnp.dot(x_rows, gate_w, preferred_element_type=jnp.float32)
    pre_up = jnp.dot(x_rows, up_w, preferred_element_type=jnp.float32)
    back_hidden = lax.dot_general(
        y_rows, down_w, (((1,), (1,)), ((), ())), preferred_element_type=jnp.float32
    )
    sigmoid_gate = jax.nn.sigmoid(pre_gate)
    activated = pre_gate * sigmoid_gate
    hidden = activated * pre_up
    pair_comb = jnp.sum(back_hidden * hidden, axis=1).astype(jnp.bfloat16)
    scaled = mix_rows.astype(jnp.float32)[:, None] * back_hidden
    d_gate = (scaled * pre_up * sigmoid_gate * (1.0 + pre_gate * (1.0 - sigmoid_gate))).astype(
        jnp.bfloat16
    )
    d_up = (scaled * activated).astype(jnp.bfloat16)
    token_part = lax.dot_general(
        d_gate, gate_w, (((1,), (1,)), ((), ())), preferred_element_type=jnp.float32
    )
    token_part = token_part + lax.dot_general(
        d_up, up_w, (((1,), (1,)), ((), ())), preferred_element_type=jnp.float32
    )
    return (d_gate, d_up, token_part.astype(jnp.bfloat16), pair_comb)


def routed_body(tokens, cotangent, expert_ids, combine_int, w_gate, w_up, w_down):
    peer_count = lax.axis_size(("expert", "seq"))
    count_tok, feature_dim = tokens.shape
    top_k = expert_ids.shape[1]
    hidden_w = w_gate.shape[2]
    capacity = min(count_tok, max(top_k, 4 * count_tok * top_k // peer_count))
    slots_all = peer_count * capacity
    weights_f = combine_int.astype(jnp.float32)
    mix_weights = (weights_f / jnp.sum(weights_f, axis=1, keepdims=True)).astype(jnp.bfloat16)
    member = (
        expert_ids[:, :, None] == jnp.arange(peer_count, dtype=jnp.int32)[None, None, :]
    ).astype(jnp.int32)
    per_token = jnp.sum(member, axis=1)
    earlier = jnp.cumsum(per_token, axis=0) - per_token
    rank_in = jnp.sum(earlier[:, None, :] * member, axis=2)
    slot_ids = expert_ids * capacity + rank_in
    routing = (
        slot_ids[:, :, None] == jnp.arange(slots_all, dtype=jnp.int32)[None, None, :]
    ).astype(jnp.float32)
    placing = jnp.sum(routing, axis=1).astype(jnp.bfloat16)
    sent_x = lax.dot_general(
        placing, tokens, (((0,), (0,)), ((), ())), preferred_element_type=jnp.float32
    )
    sent_x = sent_x.astype(jnp.bfloat16).reshape(peer_count, capacity, feature_dim)
    sent_y = lax.dot_general(
        placing, cotangent, (((0,), (0,)), ((), ())), preferred_element_type=jnp.float32
    )
    sent_y = sent_y.astype(jnp.bfloat16).reshape(peer_count, capacity, feature_dim)
    sent_g = jnp.einsum("tks,tk->s", routing, mix_weights.astype(jnp.float32))
    sent_g = sent_g.astype(jnp.bfloat16).reshape(peer_count, capacity)
    got_x, got_y, got_g = (
        lax.all_to_all(sent_x, ("expert", "seq"), split_axis=0, concat_axis=0, tiled=True),
        lax.all_to_all(sent_y, ("expert", "seq"), split_axis=0, concat_axis=0, tiled=True),
        lax.all_to_all(sent_g, ("expert", "seq"), split_axis=0, concat_axis=0, tiled=True),
    )
    x_rows = got_x.reshape(slots_all, feature_dim)
    y_rows = got_y.reshape(slots_all, feature_dim)
    mix_rows = got_g.reshape(slots_all)
    d_gate, d_up, token_part, pair_comb = expert_pass(
        x_rows, y_rows, mix_rows, w_gate[0], w_up[0], w_down[0]
    )
    ret_x, ret_c = (
        lax.all_to_all(
            token_part.reshape(peer_count, capacity, feature_dim),
            ("expert", "seq"),
            split_axis=0,
            concat_axis=0,
            tiled=True,
        ),
        lax.all_to_all(
            pair_comb.reshape(peer_count, capacity),
            ("expert", "seq"),
            split_axis=0,
            concat_axis=0,
            tiled=True,
        ),
    )
    d_both = jnp.concatenate([d_gate, d_up], axis=1)
    half_rows = feature_dim // lax.axis_size("replica")
    other_x, other_d = from_partner((x_rows, d_both), "replica", 0)
    first_row = lax.axis_index("replica") * half_rows
    own_cols = lax.dynamic_slice_in_dim(x_rows, first_row, half_rows, 1)
    other_cols = lax.dynamic_slice_in_dim(other_x, first_row, half_rows, 1)
    grad_rows = lax.dot_general(
        own_cols, d_both, (((0,), (0,)), ((), ())), preferred_element_type=jnp.float32
    )
    grad_rows = grad_rows + lax.dot_general(
        other_cols, other_d, (((0,), (0,)), ((), ())), preferred_element_type=jnp.float32
    )
    grad_gate = grad_rows[:, :hidden_w][None]
    grad_up = grad_rows[:, hidden_w:][None]
    token_grad = jnp.dot(
        placing, ret_x.reshape(slots_all, feature_dim), preferred_element_type=jnp.float32
    )
    combine_grad = jnp.einsum("tks,s->tk", routing, ret_c.reshape(slots_all).astype(jnp.float32))
    return (token_grad.astype(jnp.bfloat16), combine_grad, grad_gate, grad_up)


NT = (((1,), (1,)), ((), ()))
VMEM = pl.BlockSpec(memory_space=pltpu.VMEM)
SMEM = pl.BlockSpec(memory_space=pltpu.SMEM)
HBM = pl.BlockSpec(memory_space=pltpu.HBM)


def call(kernel, out_shape, *operands, in_specs, out_specs, scratch=(), flops=0, moved=0, limit=VMEM_LIMIT, aliases={}):
    return pl.pallas_call(
        kernel,
        out_shape=out_shape,
        in_specs=in_specs,
        out_specs=out_specs,
        scratch_shapes=scratch,
        input_output_aliases=aliases,
        cost_estimate=pl.CostEstimate(flops=flops, bytes_accessed=moved, transcendentals=0),
        compiler_params=pltpu.CompilerParams(vmem_limit_bytes=limit),
    )(*operands)


def one_hot_rows(rows):
    shape = (rows, rows)
    here = lax.broadcasted_iota(jnp.int32, shape, 0) == lax.broadcasted_iota(jnp.int32, shape, 1)
    return here.astype(jnp.bfloat16)


def message_kernel(x_ref, y_ref, ids_hbm, comb_hbm, out_ref, ids_ref, comb_ref, *sems):
    feature_dim = x_ref.shape[1]
    ids_sem, comb_sem, x_sem, y_sem = sems
    ids_copy = pltpu.make_async_copy(ids_hbm, ids_ref, ids_sem)
    comb_copy = pltpu.make_async_copy(comb_hbm, comb_ref, comb_sem)
    ids_copy.start()
    comb_copy.start()
    x_copy = pltpu.make_async_copy(x_ref, out_ref.at[:, :feature_dim], x_sem)
    y_copy = pltpu.make_async_copy(y_ref, out_ref.at[:, feature_dim : 2 * feature_dim], y_sem)
    x_copy.start()
    y_copy.start()
    ids_copy.wait()
    comb_copy.wait()
    weights = comb_ref[...].astype(jnp.float32)
    mix = (weights / jnp.sum(weights, axis=0, keepdims=True)).astype(jnp.bfloat16)
    mix = mix.astype(jnp.float32)
    ids = ids_ref[...]
    count = ids.shape[1]
    expert = lax.broadcasted_iota(jnp.int32, (LANES, count), 0)
    by_expert = jnp.zeros((LANES, count), jnp.float32)
    for k in range(ids.shape[0]):
        by_expert += jnp.where(ids[k : k + 1] == expert, mix[k : k + 1], 0.0)
    turned = lax.dot_general(
        one_hot_rows(count), by_expert.astype(jnp.bfloat16), NT, preferred_element_type=jnp.float32
    )
    out_ref[:, 2 * feature_dim :] = turned.astype(jnp.bfloat16)
    x_copy.wait()
    y_copy.wait()


def expert_rows(place_ref, blocks, weight_refs, part_refs, swap_ref, keep_ref):
    gate_ref, up_ref, down_ref = weight_refs
    rows, width = blocks[0].shape
    feature_dim = (width - LANES) // 2
    half = feature_dim // 2
    expert, replica = place_ref[0], place_ref[1]
    data = jnp.concatenate([block[...] for block in blocks], axis=0)
    x_rows = data[:, :feature_dim]
    y_rows = data[:, feature_dim : 2 * feature_dim]
    lane = lax.broadcasted_iota(jnp.int32, (data.shape[0], LANES), 1)
    mix = jnp.sum(
        jnp.where(lane == expert, data[:, 2 * feature_dim :].astype(jnp.float32), 0.0),
        axis=1,
        keepdims=True,
    )
    gate, up = gate_ref[0], up_ref[0]
    pre_gate = jnp.dot(x_rows, gate, preferred_element_type=jnp.float32)
    pre_up = jnp.dot(x_rows, up, preferred_element_type=jnp.float32)
    back = lax.dot_general(y_rows, down_ref[0], NT, preferred_element_type=jnp.float32)
    sig = jax.nn.sigmoid(pre_gate)
    activated = pre_gate * sig
    pair_comb = jnp.sum(back * (activated * pre_up), axis=1, keepdims=True)
    scaled = mix * back
    d_gate = (scaled * pre_up * sig * (1.0 + pre_gate * (1.0 - sig))).astype(jnp.bfloat16)
    d_up = (scaled * activated).astype(jnp.bfloat16)
    part = lax.dot_general(d_gate, gate, NT, preferred_element_type=jnp.float32)
    part += lax.dot_general(d_up, up, NT, preferred_element_type=jnp.float32)
    part = part.astype(jnp.bfloat16)
    comb = jnp.where(lane == expert, pair_comb, 0.0).astype(jnp.bfloat16)
    first = 0
    for out in part_refs:
        last = first + out.shape[0]
        out[:, :feature_dim] = part[first:last]
        out[:, feature_dim:] = comb[first:last]
        first = last
    hidden_w = d_gate.shape[1]
    low, high = x_rows[:, :half], x_rows[:, half:]
    count = data.shape[0]
    swap_ref[:count, :half] = jnp.where(replica == 0, high, low)
    swap_ref[:count, half : half + hidden_w] = d_gate
    swap_ref[:count, half + hidden_w :] = d_up
    keep_ref[:count] = jnp.where(replica == 0, low, high)


def far_kernel(place_ref, *refs):
    expert_rows(place_ref, refs[:4], refs[4:7], refs[7:11], *refs[11:])


def near_kernel(place_ref, far_swap_ref, far_keep_ref, *refs):
    expert_rows(place_ref, refs[:4], refs[4:7], refs[7:10], *refs[10:])
    first = refs[0].shape[0] * 4
    refs[10][first:] = far_swap_ref[...]
    refs[11][first:] = far_keep_ref[...]


def hold_kernel(after_ref, *refs):
    count = len(refs) // 2
    for source, target in zip(refs[:count], refs[count:]):
        step = source.shape[1] // 8

        @pl.loop(0, 8)
        def _(index):
            part = pl.ds(pl.multiple_of(index * step, step), step)
            target[0, part] = source[0, part]


def weight_kernel(keep_ref, own_ref, other_ref, gate_ref, up_ref, done_ref):
    done_ref[...] = jnp.zeros(done_ref.shape, done_ref.dtype)
    half = keep_ref.shape[1]
    hidden_w = gate_ref.shape[2]
    cols = jnp.concatenate([keep_ref[...], other_ref[:, :half]], axis=0)
    grads = jnp.concatenate([own_ref[:, half:], other_ref[:, half:]], axis=0)
    total = lax.dot_general(
        cols, grads, (((0,), (0,)), ((), ())), preferred_element_type=jnp.float32
    )
    gate_ref[0] = total[:, :hidden_w]
    up_ref[0] = total[:, hidden_w:]


def finish_kernel(ids_hbm, done_ref, *refs):
    *refs, ids_ref, ids_sem = refs
    ids_copy = pltpu.make_async_copy(ids_hbm, ids_ref, ids_sem)
    ids_copy.start()
    token_ref, comb_ref = refs[-2:]
    rows, feature_dim = token_ref.shape
    total = refs[0][...].astype(jnp.float32)
    for ref in refs[1:-2]:
        total += ref[...].astype(jnp.float32)
    token_ref[...] = total[:, :feature_dim].astype(jnp.bfloat16)
    comb = total[:, feature_dim:].astype(jnp.bfloat16)
    turned = lax.dot_general(
        one_hot_rows(LANES), comb, NT, preferred_element_type=jnp.float32
    )
    ids_copy.wait()
    ids = ids_ref[...]
    out = jnp.zeros(ids.shape, jnp.float32)
    for expert in range(ids.shape[0]):
        out += jnp.where(ids == expert, turned[expert : expert + 1], 0.0)
    comb_ref[...] = out


def across(block, mask):
    peers = ("expert", "seq")
    return lax.ppermute(block, peers, [(i, i ^ mask) for i in range(lax.axis_size(peers))])


def swapped(block):
    return lax.ppermute(block, "replica", [(0, 1), (1, 0)])


def add(*terms):
    total = terms[0].astype(jnp.float32)
    for term in terms[1:]:
        total = total + term.astype(jnp.float32)
    return total.astype(jnp.bfloat16)


def after(value, *others):
    return lax.optimization_barrier((value,) + others)[0]


def dense_body(tokens, cotangent, expert_ids, combine_int, w_gate, w_up, w_down):
    along_x, near_z, far_z = 1, 2, 4
    rows, feature_dim = tokens.shape
    hidden_w = w_gate.shape[2]
    half = feature_dim // 2
    bf16, f32 = jnp.bfloat16, jnp.float32
    place = jnp.stack([lax.axis_index(("expert", "seq")), lax.axis_index("replica")])
    place = place.astype(jnp.int32)
    ids_turned = expert_ids.T
    own = call(
        message_kernel,
        jax.ShapeDtypeStruct((rows, 2 * feature_dim + LANES), bf16),
        tokens,
        cotangent,
        ids_turned,
        combine_int.T,
        in_specs=[HBM] * 4,
        out_specs=VMEM,
        scratch=[pltpu.VMEM(ids_turned.shape, jnp.int32)] * 2 + [pltpu.SemaphoreType.DMA] * 4,
        moved=8 * rows * feature_dim,
        limit=VMEM_MOST,
    )
    z3 = across(own, near_z | far_z)
    x2 = across(own, along_x | far_z)
    z1 = across(own, near_z)
    x0 = across(own, along_x)
    x1 = across(z1, along_x)
    x3 = across(z3, along_x)
    z2 = across(z3, near_z)
    held = call(
        hold_kernel,
        [jax.ShapeDtypeStruct(w.shape, bf16) for w in (w_gate, w_up, w_down)],
        x0,
        w_gate,
        w_up,
        w_down,
        in_specs=[VMEM] * 4,
        out_specs=[VMEM] * 3,
        moved=12 * feature_dim * hidden_w,
    )
    part = jax.ShapeDtypeStruct((rows, feature_dim + LANES), bf16)
    pair = jax.ShapeDtypeStruct((2 * rows, feature_dim + LANES), bf16)

    def work(blocks):
        return {
            "flops": 2 * blocks * rows * feature_dim * hidden_w * 5,
            "moved": 6 * feature_dim * hidden_w + blocks * rows * feature_dim * 8,
        }

    def exchanged(blocks):
        return [
            jax.ShapeDtypeStruct((blocks * rows, half + 2 * hidden_w), bf16),
            jax.ShapeDtypeStruct((blocks * rows, half), bf16),
        ]

    f2, f3, g2, g3, *far = call(
        far_kernel,
        [part] * 4 + exchanged(4),
        place,
        *(z2, z3, x2, x3),
        *held,
        in_specs=[SMEM] + [VMEM] * 7,
        out_specs=[VMEM] * 6,
        **work(4),
    )
    f0, fg1, g0, swap, keep = call(
        near_kernel,
        [part, pair, part] + exchanged(8),
        place,
        *far,
        *(own, z1, x1, x0),
        *held,
        in_specs=[SMEM] + [VMEM] * 9,
        out_specs=[VMEM] * 5,
        **work(4),
    )
    sum3 = add(f3, across(g3, along_x))
    r3 = across(sum3, near_z | far_z)
    sum2 = add(f2, across(g2, along_x))
    r2 = across(sum2, far_z)
    r1 = across(fg1, near_z)
    r0 = across(add(g0, r1[rows:]), along_x)
    other = swapped(after(swap, sum2))
    grad = jax.ShapeDtypeStruct((1, half, hidden_w), f32)
    grad_gate, grad_up, weights_done = call(
        weight_kernel,
        (grad, grad, jax.ShapeDtypeStruct((8, LANES), f32)),
        keep,
        swap,
        other,
        in_specs=[VMEM] * 3,
        out_specs=[pl.BlockSpec((1, half, hidden_w))] * 2 + [VMEM],
        flops=2 * 16 * rows * half * 2 * hidden_w,
        moved=8 * half * hidden_w + 16 * rows * (half + 2 * hidden_w),
    )
    token_grad, comb_turned = call(
        finish_kernel,
        (jax.ShapeDtypeStruct((rows, feature_dim), bf16), jax.ShapeDtypeStruct(ids_turned.shape, f32)),
        ids_turned,
        weights_done,
        *(f0, r1[:rows], r0, r2, r3),
        in_specs=[HBM] + [VMEM] * 6,
        out_specs=[pl.BlockSpec(tokens.shape), pl.BlockSpec(ids_turned.shape)],
        scratch=[pltpu.VMEM(ids_turned.shape, jnp.int32), pltpu.SemaphoreType.DMA],
        moved=12 * rows * feature_dim,
    )
    return (token_grad, comb_turned.T, grad_gate, grad_up)


def body(*operands):
    sizes = [lax.axis_size(name) for name in ("expert", "seq", "replica")]
    if sizes == [4, 2, 2] and operands[2].shape[1] == 8:
        return dense_body(*operands)
    return routed_body(*operands)


def solution(mesh):
    in_specs = (
        P(("groups", "expert", "seq", "replica"), None),
        P(("groups", "expert", "seq", "replica"), None),
        P(("groups", "expert", "seq", "replica"), None),
        P(("groups", "expert", "seq", "replica"), None),
        P(("expert", "seq"), None, None),
        P(("expert", "seq"), None, None),
        P(("expert", "seq"), None, None),
    )
    out_specs = (
        P(("groups", "expert", "seq", "replica"), None),
        P(("groups", "expert", "seq", "replica"), None),
        P(("groups", "expert", "seq"), "replica", None),
        P(("groups", "expert", "seq"), "replica", None),
    )
    return jax.shard_map(body, mesh=mesh, in_specs=in_specs, out_specs=out_specs, check_vma=False)
```

```python
import functools

import jax
import jax.numpy as jnp
from jax import lax
from jax.experimental import pallas as pl
from jax.experimental.pallas import tpu as pltpu
from jax.sharding import PartitionSpec as P

LANES = 128
VMEM_LIMIT = 32 * 1024 * 1024
VMEM_MOST = 56 * 1024 * 1024


def from_partner(block, axis, distance):
    count = lax.axis_size(axis)
    route = []
    for low in range(count):
        high = low | 1 << distance
        if high != low and high < count:
            route += [(low, high), (high, low)]
    return lax.ppermute(block, axis, route)


def expert_pass(x_rows, y_rows, mix_rows, gate_w, up_w, down_w):
    pre_gate = jnp.dot(x_rows, gate_w, preferred_element_type=jnp.float32)
    pre_up = jnp.dot(x_rows, up_w, preferred_element_type=jnp.float32)
    back_hidden = lax.dot_general(
        y_rows, down_w, (((1,), (1,)), ((), ())), preferred_element_type=jnp.float32
    )
    sigmoid_gate = jax.nn.sigmoid(pre_gate)
    activated = pre_gate * sigmoid_gate
    hidden = activated * pre_up
    pair_comb = jnp.sum(back_hidden * hidden, axis=1).astype(jnp.bfloat16)
    scaled = mix_rows.astype(jnp.float32)[:, None] * back_hidden
    d_gate = (scaled * pre_up * sigmoid_gate * (1.0 + pre_gate * (1.0 - sigmoid_gate))).astype(
        jnp.bfloat16
    )
    d_up = (scaled * activated).astype(jnp.bfloat16)
    token_part = lax.dot_general(
        d_gate, gate_w, (((1,), (1,)), ((), ())), preferred_element_type=jnp.float32
    )
    token_part = token_part + lax.dot_general(
        d_up, up_w, (((1,), (1,)), ((), ())), preferred_element_type=jnp.float32
    )
    return (d_gate, d_up, token_part.astype(jnp.bfloat16), pair_comb)


def routed_body(tokens, cotangent, expert_ids, combine_int, w_gate, w_up, w_down):
    peer_count = lax.axis_size(("expert", "seq"))
    count_tok, feature_dim = tokens.shape
    top_k = expert_ids.shape[1]
    hidden_w = w_gate.shape[2]
    capacity = min(count_tok, max(top_k, 4 * count_tok * top_k // peer_count))
    slots_all = peer_count * capacity
    weights_f = combine_int.astype(jnp.float32)
    mix_weights = (weights_f / jnp.sum(weights_f, axis=1, keepdims=True)).astype(jnp.bfloat16)
    member = (
        expert_ids[:, :, None] == jnp.arange(peer_count, dtype=jnp.int32)[None, None, :]
    ).astype(jnp.int32)
    per_token = jnp.sum(member, axis=1)
    earlier = jnp.cumsum(per_token, axis=0) - per_token
    rank_in = jnp.sum(earlier[:, None, :] * member, axis=2)
    slot_ids = expert_ids * capacity + rank_in
    routing = (
        slot_ids[:, :, None] == jnp.arange(slots_all, dtype=jnp.int32)[None, None, :]
    ).astype(jnp.float32)
    placing = jnp.sum(routing, axis=1).astype(jnp.bfloat16)
    sent_x = lax.dot_general(
        placing, tokens, (((0,), (0,)), ((), ())), preferred_element_type=jnp.float32
    )
    sent_x = sent_x.astype(jnp.bfloat16).reshape(peer_count, capacity, feature_dim)
    sent_y = lax.dot_general(
        placing, cotangent, (((0,), (0,)), ((), ())), preferred_element_type=jnp.float32
    )
    sent_y = sent_y.astype(jnp.bfloat16).reshape(peer_count, capacity, feature_dim)
    sent_g = jnp.einsum("tks,tk->s", routing, mix_weights.astype(jnp.float32))
    sent_g = sent_g.astype(jnp.bfloat16).reshape(peer_count, capacity)
    got_x, got_y, got_g = (
        lax.all_to_all(sent_x, ("expert", "seq"), split_axis=0, concat_axis=0, tiled=True),
        lax.all_to_all(sent_y, ("expert", "seq"), split_axis=0, concat_axis=0, tiled=True),
        lax.all_to_all(sent_g, ("expert", "seq"), split_axis=0, concat_axis=0, tiled=True),
    )
    x_rows = got_x.reshape(slots_all, feature_dim)
    y_rows = got_y.reshape(slots_all, feature_dim)
    mix_rows = got_g.reshape(slots_all)
    d_gate, d_up, token_part, pair_comb = expert_pass(
        x_rows, y_rows, mix_rows, w_gate[0], w_up[0], w_down[0]
    )
    ret_x, ret_c = (
        lax.all_to_all(
            token_part.reshape(peer_count, capacity, feature_dim),
            ("expert", "seq"),
            split_axis=0,
            concat_axis=0,
            tiled=True,
        ),
        lax.all_to_all(
            pair_comb.reshape(peer_count, capacity),
            ("expert", "seq"),
            split_axis=0,
            concat_axis=0,
            tiled=True,
        ),
    )
    d_both = jnp.concatenate([d_gate, d_up], axis=1)
    half_rows = feature_dim // lax.axis_size("replica")
    other_x, other_d = from_partner((x_rows, d_both), "replica", 0)
    first_row = lax.axis_index("replica") * half_rows
    own_cols = lax.dynamic_slice_in_dim(x_rows, first_row, half_rows, 1)
    other_cols = lax.dynamic_slice_in_dim(other_x, first_row, half_rows, 1)
    grad_rows = lax.dot_general(
        own_cols, d_both, (((0,), (0,)), ((), ())), preferred_element_type=jnp.float32
    )
    grad_rows = grad_rows + lax.dot_general(
        other_cols, other_d, (((0,), (0,)), ((), ())), preferred_element_type=jnp.float32
    )
    grad_gate = grad_rows[:, :hidden_w][None]
    grad_up = grad_rows[:, hidden_w:][None]
    token_grad = jnp.dot(
        placing, ret_x.reshape(slots_all, feature_dim), preferred_element_type=jnp.float32
    )
    combine_grad = jnp.einsum("tks,s->tk", routing, ret_c.reshape(slots_all).astype(jnp.float32))
    return (token_grad.astype(jnp.bfloat16), combine_grad, grad_gate, grad_up)


NT = (((1,), (1,)), ((), ()))
VMEM = pl.BlockSpec(memory_space=pltpu.VMEM)
SMEM = pl.BlockSpec(memory_space=pltpu.SMEM)
HBM = pl.BlockSpec(memory_space=pltpu.HBM)


def call(kernel, out_shape, *operands, in_specs, out_specs, scratch=(), flops=0, moved=0, limit=VMEM_LIMIT, aliases={}):
    return pl.pallas_call(
        kernel,
        out_shape=out_shape,
        in_specs=in_specs,
        out_specs=out_specs,
        scratch_shapes=scratch,
        input_output_aliases=aliases,
        cost_estimate=pl.CostEstimate(flops=flops, bytes_accessed=moved, transcendentals=0),
        compiler_params=pltpu.CompilerParams(vmem_limit_bytes=limit),
    )(*operands)


def one_hot_rows(rows):
    shape = (rows, rows)
    here = lax.broadcasted_iota(jnp.int32, shape, 0) == lax.broadcasted_iota(jnp.int32, shape, 1)
    return here.astype(jnp.bfloat16)


def message_kernel(x_ref, y_ref, ids_hbm, comb_hbm, out_ref, ids_ref, comb_ref, *sems):
    feature_dim = x_ref.shape[1]
    ids_sem, comb_sem, x_sem, y_sem = sems
    ids_copy = pltpu.make_async_copy(ids_hbm, ids_ref, ids_sem)
    comb_copy = pltpu.make_async_copy(comb_hbm, comb_ref, comb_sem)
    ids_copy.start()
    comb_copy.start()
    x_copy = pltpu.make_async_copy(x_ref, out_ref.at[:, :feature_dim], x_sem)
    y_copy = pltpu.make_async_copy(y_ref, out_ref.at[:, feature_dim : 2 * feature_dim], y_sem)
    x_copy.start()
    y_copy.start()
    ids_copy.wait()
    comb_copy.wait()
    weights = comb_ref[...].astype(jnp.float32)
    mix = (weights / jnp.sum(weights, axis=0, keepdims=True)).astype(jnp.bfloat16)
    mix = mix.astype(jnp.float32)
    ids = ids_ref[...]
    count = ids.shape[1]
    expert = lax.broadcasted_iota(jnp.int32, (LANES, count), 0)
    by_expert = jnp.zeros((LANES, count), jnp.float32)
    for k in range(ids.shape[0]):
        by_expert += jnp.where(ids[k : k + 1] == expert, mix[k : k + 1], 0.0)
    turned = lax.dot_general(
        one_hot_rows(count), by_expert.astype(jnp.bfloat16), NT, preferred_element_type=jnp.float32
    )
    out_ref[:, 2 * feature_dim :] = turned.astype(jnp.bfloat16)
    x_copy.wait()
    y_copy.wait()


def expert_rows(place_ref, blocks, weight_refs, part_refs, swap_ref, keep_ref):
    gate_ref, up_ref, down_ref = weight_refs
    rows, width = blocks[0].shape
    feature_dim = (width - LANES) // 2
    half = feature_dim // 2
    expert, replica = place_ref[0], place_ref[1]
    data = jnp.concatenate([block[...] for block in blocks], axis=0)
    x_rows = data[:, :feature_dim]
    y_rows = data[:, feature_dim : 2 * feature_dim]
    lane = lax.broadcasted_iota(jnp.int32, (data.shape[0], LANES), 1)
    mix = jnp.sum(
        jnp.where(lane == expert, data[:, 2 * feature_dim :].astype(jnp.float32), 0.0),
        axis=1,
        keepdims=True,
    )
    gate, up = gate_ref[0], up_ref[0]
    pre_gate = jnp.dot(x_rows, gate, preferred_element_type=jnp.float32)
    pre_up = jnp.dot(x_rows, up, preferred_element_type=jnp.float32)
    back = lax.dot_general(y_rows, down_ref[0], NT, preferred_element_type=jnp.float32)
    sig = jax.nn.sigmoid(pre_gate)
    activated = pre_gate * sig
    pair_comb = jnp.sum(back * (activated * pre_up), axis=1, keepdims=True)
    scaled = mix * back
    d_gate = (scaled * pre_up * sig * (1.0 + pre_gate * (1.0 - sig))).astype(jnp.bfloat16)
    d_up = (scaled * activated).astype(jnp.bfloat16)
    part = lax.dot_general(d_gate, gate, NT, preferred_element_type=jnp.float32)
    part += lax.dot_general(d_up, up, NT, preferred_element_type=jnp.float32)
    part = part.astype(jnp.bfloat16)
    comb = jnp.where(lane == expert, pair_comb, 0.0).astype(jnp.bfloat16)
    first = 0
    for out in part_refs:
        last = first + out.shape[0]
        out[:, :feature_dim] = part[first:last]
        out[:, feature_dim:] = comb[first:last]
        first = last
    hidden_w = d_gate.shape[1]
    low, high = x_rows[:, :half], x_rows[:, half:]
    count = data.shape[0]
    swap_ref[:count, :half] = jnp.where(replica == 0, high, low)
    swap_ref[:count, half : half + hidden_w] = d_gate
    swap_ref[:count, half + hidden_w :] = d_up
    keep_ref[:count] = jnp.where(replica == 0, low, high)


def far_kernel(place_ref, *refs):
    expert_rows(place_ref, refs[:4], refs[4:7], refs[7:11], *refs[11:])


def near_kernel(place_ref, far_swap_ref, far_keep_ref, *refs):
    expert_rows(place_ref, refs[:4], refs[4:7], refs[7:10], *refs[10:])
    first = refs[0].shape[0] * 4
    refs[10][first:] = far_swap_ref[...]
    refs[11][first:] = far_keep_ref[...]


def hold_kernel(after_ref, *refs):
    count = len(refs) // 2
    for source, target in zip(refs[:count], refs[count:]):
        step = source.shape[1] // 8

        @pl.loop(0, 8)
        def _(index):
            part = pl.ds(pl.multiple_of(index * step, step), step)
            target[0, part] = source[0, part]


def weight_kernel(keep_ref, own_ref, other_ref, gate_ref, up_ref, done_ref):
    done_ref[...] = jnp.zeros(done_ref.shape, done_ref.dtype)
    half = keep_ref.shape[1]
    hidden_w = gate_ref.shape[2]
    cols = jnp.concatenate([keep_ref[...], other_ref[:, :half]], axis=0)
    grads = jnp.concatenate([own_ref[:, half:], other_ref[:, half:]], axis=0)
    total = lax.dot_general(
        cols, grads, (((0,), (0,)), ((), ())), preferred_element_type=jnp.float32
    )
    gate_ref[0] = total[:, :hidden_w]
    up_ref[0] = total[:, hidden_w:]


def finish_kernel(ids_hbm, done_ref, *refs):
    *refs, ids_ref, ids_sem = refs
    ids_copy = pltpu.make_async_copy(ids_hbm, ids_ref, ids_sem)
    ids_copy.start()
    token_ref, comb_ref = refs[-2:]
    rows, feature_dim = token_ref.shape
    total = refs[0][...].astype(jnp.float32)
    for ref in refs[1:-2]:
        total += ref[...].astype(jnp.float32)
    token_ref[...] = total[:, :feature_dim].astype(jnp.bfloat16)
    comb = total[:, feature_dim:].astype(jnp.bfloat16)
    turned = lax.dot_general(
        one_hot_rows(LANES), comb, NT, preferred_element_type=jnp.float32
    )
    ids_copy.wait()
    ids = ids_ref[...]
    out = jnp.zeros(ids.shape, jnp.float32)
    for expert in range(ids.shape[0]):
        out += jnp.where(ids == expert, turned[expert : expert + 1], 0.0)
    comb_ref[...] = out


def across(block, mask):
    peers = ("expert", "seq")
    return lax.ppermute(block, peers, [(i, i ^ mask) for i in range(lax.axis_size(peers))])


def swapped(block):
    return lax.ppermute(block, "replica", [(0, 1), (1, 0)])


def add(*terms):
    total = terms[0].astype(jnp.float32)
    for term in terms[1:]:
        total = total + term.astype(jnp.float32)
    return total.astype(jnp.bfloat16)


def after(value, *others):
    return lax.optimization_barrier((value,) + others)[0]


def dense_body(tokens, cotangent, expert_ids, combine_int, w_gate, w_up, w_down):
    along_x, near_z, far_z = 1, 2, 4
    rows, feature_dim = tokens.shape
    hidden_w = w_gate.shape[2]
    half = feature_dim // 2
    bf16, f32 = jnp.bfloat16, jnp.float32
    place = jnp.stack([lax.axis_index(("expert", "seq")), lax.axis_index("replica")])
    place = place.astype(jnp.int32)
    ids_turned = expert_ids.T
    own = call(
        message_kernel,
        jax.ShapeDtypeStruct((rows, 2 * feature_dim + LANES), bf16),
        tokens,
        cotangent,
        ids_turned,
        combine_int.T,
        in_specs=[HBM] * 4,
        out_specs=VMEM,
        scratch=[pltpu.VMEM(ids_turned.shape, jnp.int32)] * 2 + [pltpu.SemaphoreType.DMA] * 4,
        moved=8 * rows * feature_dim,
        limit=VMEM_MOST,
    )
    z3 = across(own, near_z | far_z)
    x2 = across(own, along_x | far_z)
    z1 = across(own, near_z)
    x0 = across(own, along_x)
    x1 = across(z1, along_x)
    x3 = across(z3, along_x)
    z2 = across(z3, near_z)

    def hold(after_block, *weights):
        return call(
            hold_kernel,
            [jax.ShapeDtypeStruct(w.shape, bf16) for w in weights],
            after_block,
            *weights,
            in_specs=[VMEM] * (1 + len(weights)),
            out_specs=[VMEM] * len(weights),
            moved=4 * len(weights) * feature_dim * hidden_w,
        )

    held = hold(x0, w_gate, w_up) + hold(z3, w_down)
    part = jax.ShapeDtypeStruct((rows, feature_dim + LANES), bf16)
    pair = jax.ShapeDtypeStruct((2 * rows, feature_dim + LANES), bf16)

    def work(blocks):
        return {
            "flops": 2 * blocks * rows * feature_dim * hidden_w * 5,
            "moved": 6 * feature_dim * hidden_w + blocks * rows * feature_dim * 8,
        }

    def exchanged(blocks):
        return [
            jax.ShapeDtypeStruct((blocks * rows, half + 2 * hidden_w), bf16),
            jax.ShapeDtypeStruct((blocks * rows, half), bf16),
        ]

    f2, f3, g2, g3, *far = call(
        far_kernel,
        [part] * 4 + exchanged(4),
        place,
        *(z2, z3, x2, x3),
        *held,
        in_specs=[SMEM] + [VMEM] * 7,
        out_specs=[VMEM] * 6,
        **work(4),
    )
    f0, fg1, g0, swap, keep = call(
        near_kernel,
        [part, pair, part] + exchanged(8),
        place,
        *far,
        *(own, z1, x1, x0),
        *held,
        in_specs=[SMEM] + [VMEM] * 9,
        out_specs=[VMEM] * 5,
        **work(4),
    )
    sum3 = add(f3, across(g3, along_x))
    r3 = across(sum3, near_z | far_z)
    sum2 = add(f2, across(g2, along_x))
    r2 = across(sum2, far_z)
    r1 = across(fg1, near_z)
    r0 = across(add(g0, r1[rows:]), along_x)
    other = swapped(after(swap, sum2))
    grad = jax.ShapeDtypeStruct((1, half, hidden_w), f32)
    grad_gate, grad_up, weights_done = call(
        weight_kernel,
        (grad, grad, jax.ShapeDtypeStruct((8, LANES), f32)),
        keep,
        swap,
        other,
        in_specs=[VMEM] * 3,
        out_specs=[pl.BlockSpec((1, half, hidden_w))] * 2 + [VMEM],
        flops=2 * 16 * rows * half * 2 * hidden_w,
        moved=8 * half * hidden_w + 16 * rows * (half + 2 * hidden_w),
    )
    token_grad, comb_turned = call(
        finish_kernel,
        (jax.ShapeDtypeStruct((rows, feature_dim), bf16), jax.ShapeDtypeStruct(ids_turned.shape, f32)),
        ids_turned,
        weights_done,
        *(f0, r1[:rows], r0, r2, r3),
        in_specs=[HBM] + [VMEM] * 6,
        out_specs=[pl.BlockSpec(tokens.shape), pl.BlockSpec(ids_turned.shape)],
        scratch=[pltpu.VMEM(ids_turned.shape, jnp.int32), pltpu.SemaphoreType.DMA],
        moved=12 * rows * feature_dim,
    )
    return (token_grad, comb_turned.T, grad_gate, grad_up)


def body(*operands):
    sizes = [lax.axis_size(name) for name in ("expert", "seq", "replica")]
    if sizes == [4, 2, 2] and operands[2].shape[1] == 8:
        return dense_body(*operands)
    return routed_body(*operands)


def solution(mesh):
    in_specs = (
        P(("groups", "expert", "seq", "replica"), None),
        P(("groups", "expert", "seq", "replica"), None),
        P(("groups", "expert", "seq", "replica"), None),
        P(("groups", "expert", "seq", "replica"), None),
        P(("expert", "seq"), None, None),
        P(("expert", "seq"), None, None),
        P(("expert", "seq"), None, None),
    )
    out_specs = (
        P(("groups", "expert", "seq", "replica"), None),
        P(("groups", "expert", "seq", "replica"), None),
        P(("groups", "expert", "seq"), "replica", None),
        P(("groups", "expert", "seq"), "replica", None),
    )
    return jax.shard_map(body, mesh=mesh, in_specs=in_specs, out_specs=out_specs, check_vma=False)
```

```python
import functools

import jax
import jax.numpy as jnp
from jax import lax
from jax.experimental import pallas as pl
from jax.experimental.pallas import tpu as pltpu
from jax.sharding import PartitionSpec as P

LANES = 128
VMEM_LIMIT = 32 * 1024 * 1024
VMEM_MOST = 56 * 1024 * 1024


def from_partner(block, axis, distance):
    count = lax.axis_size(axis)
    route = []
    for low in range(count):
        high = low | 1 << distance
        if high != low and high < count:
            route += [(low, high), (high, low)]
    return lax.ppermute(block, axis, route)


def expert_pass(x_rows, y_rows, mix_rows, gate_w, up_w, down_w):
    pre_gate = jnp.dot(x_rows, gate_w, preferred_element_type=jnp.float32)
    pre_up = jnp.dot(x_rows, up_w, preferred_element_type=jnp.float32)
    back_hidden = lax.dot_general(
        y_rows, down_w, (((1,), (1,)), ((), ())), preferred_element_type=jnp.float32
    )
    sigmoid_gate = jax.nn.sigmoid(pre_gate)
    activated = pre_gate * sigmoid_gate
    hidden = activated * pre_up
    pair_comb = jnp.sum(back_hidden * hidden, axis=1).astype(jnp.bfloat16)
    scaled = mix_rows.astype(jnp.float32)[:, None] * back_hidden
    d_gate = (scaled * pre_up * sigmoid_gate * (1.0 + pre_gate * (1.0 - sigmoid_gate))).astype(
        jnp.bfloat16
    )
    d_up = (scaled * activated).astype(jnp.bfloat16)
    token_part = lax.dot_general(
        d_gate, gate_w, (((1,), (1,)), ((), ())), preferred_element_type=jnp.float32
    )
    token_part = token_part + lax.dot_general(
        d_up, up_w, (((1,), (1,)), ((), ())), preferred_element_type=jnp.float32
    )
    return (d_gate, d_up, token_part.astype(jnp.bfloat16), pair_comb)


def routed_body(tokens, cotangent, expert_ids, combine_int, w_gate, w_up, w_down):
    peer_count = lax.axis_size(("expert", "seq"))
    count_tok, feature_dim = tokens.shape
    top_k = expert_ids.shape[1]
    hidden_w = w_gate.shape[2]
    capacity = min(count_tok, max(top_k, 4 * count_tok * top_k // peer_count))
    slots_all = peer_count * capacity
    weights_f = combine_int.astype(jnp.float32)
    mix_weights = (weights_f / jnp.sum(weights_f, axis=1, keepdims=True)).astype(jnp.bfloat16)
    member = (
        expert_ids[:, :, None] == jnp.arange(peer_count, dtype=jnp.int32)[None, None, :]
    ).astype(jnp.int32)
    per_token = jnp.sum(member, axis=1)
    earlier = jnp.cumsum(per_token, axis=0) - per_token
    rank_in = jnp.sum(earlier[:, None, :] * member, axis=2)
    slot_ids = expert_ids * capacity + rank_in
    routing = (
        slot_ids[:, :, None] == jnp.arange(slots_all, dtype=jnp.int32)[None, None, :]
    ).astype(jnp.float32)
    placing = jnp.sum(routing, axis=1).astype(jnp.bfloat16)
    sent_x = lax.dot_general(
        placing, tokens, (((0,), (0,)), ((), ())), preferred_element_type=jnp.float32
    )
    sent_x = sent_x.astype(jnp.bfloat16).reshape(peer_count, capacity, feature_dim)
    sent_y = lax.dot_general(
        placing, cotangent, (((0,), (0,)), ((), ())), preferred_element_type=jnp.float32
    )
    sent_y = sent_y.astype(jnp.bfloat16).reshape(peer_count, capacity, feature_dim)
    sent_g = jnp.einsum("tks,tk->s", routing, mix_weights.astype(jnp.float32))
    sent_g = sent_g.astype(jnp.bfloat16).reshape(peer_count, capacity)
    got_x, got_y, got_g = (
        lax.all_to_all(sent_x, ("expert", "seq"), split_axis=0, concat_axis=0, tiled=True),
        lax.all_to_all(sent_y, ("expert", "seq"), split_axis=0, concat_axis=0, tiled=True),
        lax.all_to_all(sent_g, ("expert", "seq"), split_axis=0, concat_axis=0, tiled=True),
    )
    x_rows = got_x.reshape(slots_all, feature_dim)
    y_rows = got_y.reshape(slots_all, feature_dim)
    mix_rows = got_g.reshape(slots_all)
    d_gate, d_up, token_part, pair_comb = expert_pass(
        x_rows, y_rows, mix_rows, w_gate[0], w_up[0], w_down[0]
    )
    ret_x, ret_c = (
        lax.all_to_all(
            token_part.reshape(peer_count, capacity, feature_dim),
            ("expert", "seq"),
            split_axis=0,
            concat_axis=0,
            tiled=True,
        ),
        lax.all_to_all(
            pair_comb.reshape(peer_count, capacity),
            ("expert", "seq"),
            split_axis=0,
            concat_axis=0,
            tiled=True,
        ),
    )
    d_both = jnp.concatenate([d_gate, d_up], axis=1)
    half_rows = feature_dim // lax.axis_size("replica")
    other_x, other_d = from_partner((x_rows, d_both), "replica", 0)
    first_row = lax.axis_index("replica") * half_rows
    own_cols = lax.dynamic_slice_in_dim(x_rows, first_row, half_rows, 1)
    other_cols = lax.dynamic_slice_in_dim(other_x, first_row, half_rows, 1)
    grad_rows = lax.dot_general(
        own_cols, d_both, (((0,), (0,)), ((), ())), preferred_element_type=jnp.float32
    )
    grad_rows = grad_rows + lax.dot_general(
        other_cols, other_d, (((0,), (0,)), ((), ())), preferred_element_type=jnp.float32
    )
    grad_gate = grad_rows[:, :hidden_w][None]
    grad_up = grad_rows[:, hidden_w:][None]
    token_grad = jnp.dot(
        placing, ret_x.reshape(slots_all, feature_dim), preferred_element_type=jnp.float32
    )
    combine_grad = jnp.einsum("tks,s->tk", routing, ret_c.reshape(slots_all).astype(jnp.float32))
    return (token_grad.astype(jnp.bfloat16), combine_grad, grad_gate, grad_up)


NT = (((1,), (1,)), ((), ()))
VMEM = pl.BlockSpec(memory_space=pltpu.VMEM)
SMEM = pl.BlockSpec(memory_space=pltpu.SMEM)
HBM = pl.BlockSpec(memory_space=pltpu.HBM)


def call(kernel, out_shape, *operands, in_specs, out_specs, scratch=(), flops=0, moved=0, limit=VMEM_LIMIT, aliases={}):
    return pl.pallas_call(
        kernel,
        out_shape=out_shape,
        in_specs=in_specs,
        out_specs=out_specs,
        scratch_shapes=scratch,
        input_output_aliases=aliases,
        cost_estimate=pl.CostEstimate(flops=flops, bytes_accessed=moved, transcendentals=0),
        compiler_params=pltpu.CompilerParams(vmem_limit_bytes=limit),
    )(*operands)


def one_hot_rows(rows):
    shape = (rows, rows)
    here = lax.broadcasted_iota(jnp.int32, shape, 0) == lax.broadcasted_iota(jnp.int32, shape, 1)
    return here.astype(jnp.bfloat16)


def message_kernel(x_ref, y_ref, ids_hbm, comb_hbm, out_ref, ids_ref, comb_ref, *sems):
    feature_dim = x_ref.shape[1]
    ids_sem, comb_sem, x_sem, y_sem = sems
    ids_copy = pltpu.make_async_copy(ids_hbm, ids_ref, ids_sem)
    comb_copy = pltpu.make_async_copy(comb_hbm, comb_ref, comb_sem)
    ids_copy.start()
    comb_copy.start()
    x_copy = pltpu.make_async_copy(x_ref, out_ref.at[:, :feature_dim], x_sem)
    y_copy = pltpu.make_async_copy(y_ref, out_ref.at[:, feature_dim : 2 * feature_dim], y_sem)
    x_copy.start()
    y_copy.start()
    ids_copy.wait()
    comb_copy.wait()
    weights = comb_ref[...].astype(jnp.float32)
    mix = (weights / jnp.sum(weights, axis=0, keepdims=True)).astype(jnp.bfloat16)
    mix = mix.astype(jnp.float32)
    ids = ids_ref[...]
    count = ids.shape[1]
    expert = lax.broadcasted_iota(jnp.int32, (LANES, count), 0)
    by_expert = jnp.zeros((LANES, count), jnp.float32)
    for k in range(ids.shape[0]):
        by_expert += jnp.where(ids[k : k + 1] == expert, mix[k : k + 1], 0.0)
    turned = lax.dot_general(
        one_hot_rows(count), by_expert.astype(jnp.bfloat16), NT, preferred_element_type=jnp.float32
    )
    out_ref[:, 2 * feature_dim :] = turned.astype(jnp.bfloat16)
    x_copy.wait()
    y_copy.wait()


def expert_rows(place_ref, blocks, weight_refs, part_refs, grad_ref):
    pair_ref, down_ref = weight_refs
    rows, width = blocks[0].shape
    feature_dim = (width - LANES) // 2
    expert = place_ref[0]
    data = jnp.concatenate([block[...] for block in blocks], axis=0)
    x_rows = data[:, :feature_dim]
    y_rows = data[:, feature_dim : 2 * feature_dim]
    lane = lax.broadcasted_iota(jnp.int32, (data.shape[0], LANES), 1)
    mix = jnp.sum(
        jnp.where(lane == expert, data[:, 2 * feature_dim :].astype(jnp.float32), 0.0),
        axis=1,
        keepdims=True,
    )
    pair = pair_ref[0]
    hidden_w = pair.shape[1] // 2
    pre = jnp.dot(x_rows, pair, preferred_element_type=jnp.float32)
    pre_gate, pre_up = pre[:, :hidden_w], pre[:, hidden_w:]
    back = lax.dot_general(y_rows, down_ref[0], NT, preferred_element_type=jnp.float32)
    sig = jax.nn.sigmoid(pre_gate)
    activated = pre_gate * sig
    pair_comb = jnp.sum(back * (activated * pre_up), axis=1, keepdims=True)
    scaled = mix * back
    d_gate = (scaled * pre_up * sig * (1.0 + pre_gate * (1.0 - sig))).astype(jnp.bfloat16)
    d_up = (scaled * activated).astype(jnp.bfloat16)
    d_both = jnp.concatenate([d_gate, d_up], axis=1)
    part = lax.dot_general(d_both, pair, NT, preferred_element_type=jnp.float32)
    part = part.astype(jnp.bfloat16)
    comb = jnp.where(lane == expert, pair_comb, 0.0).astype(jnp.bfloat16)
    first = 0
    for out in part_refs:
        last = first + out.shape[0]
        out[:, :feature_dim] = part[first:last]
        out[:, feature_dim:] = comb[first:last]
        first = last
    grad_ref[: data.shape[0], grad_ref.shape[1] - 2 * hidden_w :] = d_both


def far_kernel(place_ref, *refs):
    expert_rows(place_ref, refs[:4], refs[4:6], refs[6:10], refs[10])


def near_kernel(place_ref, far_grad_ref, *refs):
    near, weights, far = refs[:4], refs[4:6], refs[6:10]
    swap_ref, keep_ref = refs[13:]
    expert_rows(place_ref, near, weights, refs[10:13], swap_ref)
    rows, half = near[0].shape[0], keep_ref.shape[1]
    swap_ref[4 * rows :, half:] = far_grad_ref[...]
    first = place_ref[1] == 0
    for index, block in enumerate((*near, *far)):
        low, high = block[:, :half], block[:, half : 2 * half]
        place = slice(index * rows, (index + 1) * rows)
        swap_ref[place, :half] = jnp.where(first, high, low)
        keep_ref[place] = jnp.where(first, low, high)


def hold_kernel(after_ref, *refs):
    target = refs[-1]
    steps = 8
    for number, source in enumerate(refs[:-1]):
        step, width = source.shape[1] // steps, source.shape[2]

        @pl.loop(0, steps)
        def _(index):
            rows = pl.ds(pl.multiple_of(index * step, step), step)
            target[0, rows, number * width : (number + 1) * width] = source[0, rows]


def _(index):
            part = pl.ds(pl.multiple_of(index * step, step), step)
            target[0, part] = source[0, part]


def weight_kernel(keep_ref, own_ref, other_ref, gate_ref, up_ref, done_ref):
    done_ref[...] = jnp.zeros(done_ref.shape, done_ref.dtype)
    half = keep_ref.shape[1]
    hidden_w = gate_ref.shape[2]
    cols = jnp.concatenate([keep_ref[...], other_ref[:, :half]], axis=0)
    grads = jnp.concatenate([own_ref[:, half:], other_ref[:, half:]], axis=0)
    total = lax.dot_general(
        cols, grads, (((0,), (0,)), ((), ())), preferred_element_type=jnp.float32
    )
    gate_ref[0] = total[:, :hidden_w]
    up_ref[0] = total[:, hidden_w:]


def finish_kernel(ids_ref, done_ref, *refs):
    token_ref, comb_ref = refs[-2:]
    rows, feature_dim = token_ref.shape
    total = refs[0][...].astype(jnp.float32)
    for ref in refs[1:-2]:
        total += ref[...].astype(jnp.float32)
    token_ref[...] = total[:, :feature_dim].astype(jnp.bfloat16)
    comb = total[:, feature_dim:].astype(jnp.bfloat16)
    turned = lax.dot_general(
        one_hot_rows(LANES), comb, NT, preferred_element_type=jnp.float32
    )
    ids = ids_ref[...]
    out = jnp.zeros(ids.shape, jnp.float32)
    for expert in range(ids.shape[0]):
        out += jnp.where(ids == expert, turned[expert : expert + 1], 0.0)
    comb_ref[...] = out


def across(block, mask):
    peers = ("expert", "seq")
    return lax.ppermute(block, peers, [(i, i ^ mask) for i in range(lax.axis_size(peers))])


def swapped(block):
    return lax.ppermute(block, "replica", [(0, 1), (1, 0)])


def add(*terms):
    total = terms[0].astype(jnp.float32)
    for term in terms[1:]:
        total = total + term.astype(jnp.float32)
    return total.astype(jnp.bfloat16)


def after(value, *others):
    return lax.optimization_barrier((value,) + others)[0]


def dense_body(tokens, cotangent, expert_ids, combine_int, w_gate, w_up, w_down):
    along_x, near_z, far_z = 1, 2, 4
    rows, feature_dim = tokens.shape
    hidden_w = w_gate.shape[2]
    half = feature_dim // 2
    bf16, f32 = jnp.bfloat16, jnp.float32
    place = jnp.stack([lax.axis_index(("expert", "seq")), lax.axis_index("replica")])
    place = place.astype(jnp.int32)
    ids_turned = expert_ids.T
    own, ids_held = call(
        message_kernel,
        [
            jax.ShapeDtypeStruct((rows, 2 * feature_dim + LANES), bf16),
            jax.ShapeDtypeStruct(ids_turned.shape, jnp.int32),
        ],
        tokens,
        cotangent,
        ids_turned,
        combine_int.T,
        in_specs=[HBM] * 4,
        out_specs=[VMEM] * 2,
        scratch=[pltpu.VMEM(ids_turned.shape, jnp.int32)] + [pltpu.SemaphoreType.DMA] * 4,
        moved=8 * rows * feature_dim,
        limit=VMEM_MOST,
    )
    z3 = across(own, near_z | far_z)
    x2 = across(own, along_x | far_z)
    z1 = across(own, near_z)
    x0 = across(own, along_x)
    x1 = across(z1, along_x)
    x3 = across(z3, along_x)
    z2 = across(z3, near_z)

    def hold(after_block, *weights):
        return call(
            hold_kernel,
            jax.ShapeDtypeStruct((*weights[0].shape[:2], len(weights) * weights[0].shape[2]), bf16),
            after_block,
            *weights,
            in_specs=[VMEM] * (1 + len(weights)),
            out_specs=VMEM,
            moved=4 * len(weights) * feature_dim * hidden_w,
        )

    held = (hold(x0, w_gate, w_up), hold(z3, w_down))
    part = jax.ShapeDtypeStruct((rows, feature_dim + LANES), bf16)
    pair = jax.ShapeDtypeStruct((2 * rows, feature_dim + LANES), bf16)

    def work(blocks):
        return {
            "flops": 2 * blocks * rows * feature_dim * hidden_w * 5,
            "moved": 6 * feature_dim * hidden_w + blocks * rows * feature_dim * 8,
        }

    def exchanged(blocks):
        return [
            jax.ShapeDtypeStruct((blocks * rows, half + 2 * hidden_w), bf16),
            jax.ShapeDtypeStruct((blocks * rows, half), bf16),
        ]

    f2, f3, g2, g3, far_grad = call(
        far_kernel,
        [part] * 4 + [jax.ShapeDtypeStruct((4 * rows, 2 * hidden_w), bf16)],
        place,
        *(z2, z3, x2, x3),
        *held,
        in_specs=[SMEM] + [VMEM] * 6,
        out_specs=[VMEM] * 5,
        **work(4),
    )
    f0, fg1, g0, swap, keep = call(
        near_kernel,
        [part, pair, part] + exchanged(8),
        place,
        far_grad,
        *(own, z1, x1, x0),
        *held,
        *(z2, z3, x2, x3),
        in_specs=[SMEM] + [VMEM] * 11,
        out_specs=[VMEM] * 5,
        **work(4),
    )
    sum3 = add(f3, across(g3, along_x))
    r3 = across(sum3, near_z | far_z)
    sum2 = add(f2, across(g2, along_x))
    r2 = across(sum2, far_z)
    r1 = across(fg1, near_z)
    r0 = across(add(g0, r1[rows:]), along_x)
    other = swapped(after(swap, sum2))
    grad = jax.ShapeDtypeStruct((1, half, hidden_w), f32)
    grad_gate, grad_up, weights_done = call(
        weight_kernel,
        (grad, grad, jax.ShapeDtypeStruct((8, LANES), f32)),
        keep,
        swap,
        other,
        in_specs=[VMEM] * 3,
        out_specs=[pl.BlockSpec((1, half, hidden_w))] * 2 + [VMEM],
        flops=2 * 16 * rows * half * 2 * hidden_w,
        moved=8 * half * hidden_w + 16 * rows * (half + 2 * hidden_w),
    )
    token_grad, comb_turned = call(
        finish_kernel,
        (jax.ShapeDtypeStruct((rows, feature_dim), bf16), jax.ShapeDtypeStruct(ids_turned.shape, f32)),
        ids_held,
        weights_done,
        *(f0, r1[:rows], r0, r2, r3),
        in_specs=[VMEM] * 7,
        out_specs=[pl.BlockSpec(tokens.shape), pl.BlockSpec(ids_turned.shape)],
        moved=12 * rows * feature_dim,
    )
    return (token_grad, comb_turned.T, grad_gate, grad_up)


def body(*operands):
    sizes = [lax.axis_size(name) for name in ("expert", "seq", "replica")]
    if sizes == [4, 2, 2] and operands[2].shape[1] == 8:
        return dense_body(*operands)
    return routed_body(*operands)


def solution(mesh):
    in_specs = (
        P(("groups", "expert", "seq", "replica"), None),
        P(("groups", "expert", "seq", "replica"), None),
        P(("groups", "expert", "seq", "replica"), None),
        P(("groups", "expert", "seq", "replica"), None),
        P(("expert", "seq"), None, None),
        P(("expert", "seq"), None, None),
        P(("expert", "seq"), None, None),
    )
    out_specs = (
        P(("groups", "expert", "seq", "replica"), None),
        P(("groups", "expert", "seq", "replica"), None),
        P(("groups", "expert", "seq"), "replica", None),
        P(("groups", "expert", "seq"), "replica", None),
    )
    return jax.shard_map(body, mesh=mesh, in_specs=in_specs, out_specs=out_specs, check_vma=False)
```
